32 devices in a mesh: rep: 2 (over x), ep: 8 (over z, y), sub: 2 (over core).
Axes of the slice: x: 2, y: 2, z: 4, core: 2. Of those that a mesh axis runs over, the one named last changes fastest.
Arguments:
- queries: bfloat16 [512, 36864], P(('rep', 'ep', 'sub')), parts along dimension 0, may hold values from -8 to 8
- page_pool: bfloat16 [1024, 36864], P(('rep', 'ep', 'sub')), parts along dimension 0, may hold values from -8 to 8
- page_table: int32 [128, 16], P('rep'), parts along dimension 0, may hold values from 0 to 511, as said below
- serving: int32 [128], P('rep'), parts along dimension 0, may hold values from 0 to 63, as said below
- context_len: int32 [128], P('rep'), parts along dimension 0, may hold values from 256 to 1024
- residual: bfloat16 [512, 3584], P(('rep', 'ep', 'sub')), parts along dimension 0, may hold values from -6 to 6
- routes: int32 [512, 2], P(('rep', 'ep', 'sub')), parts along dimension 0, may hold values from 0 to 3, all different within a row; in each aligned block of 16 rows (0 to 15, 16 to 31, ...) at most 10 rows name the same one
- route_scores: float32 [512, 2], P(('rep', 'ep', 'sub')), parts along dimension 0, may hold values from 0.1 to 1
- w_gate: bfloat16 [8, 3584, 512], P('ep', None, 'sub'), may hold values from -0.09375 to 0.09375
- w_up: bfloat16 [8, 3584, 512], P('ep', None, 'sub'), may hold values from -0.09375 to 0.09375
- w_down: bfloat16 [8, 512, 3584], P('ep', 'sub'), may hold values from -0.1875 to 0.1875
Outputs:
- latent_out: bfloat16 [512, 32768], P(('rep', 'ep', 'sub')), parts along dimension 0
- moe_out: bfloat16 [512, 3584], P(('rep', 'ep', 'sub')), parts along dimension 0
The draws below stay inside these ranges and needn't reach their ends.
There are 2 independent parts, one for each index of `rep`. The reference program is written for one: setup_inputs(seed, part) draws one part's arguments, and reference() takes and returns one part's arrays. A program takes and returns all parts, laid end to end along the dimension named above; an argument that names none is the same for every part. Nothing has to cross between parts.
Inputs may be any that keep to these rules, and one draw needn't show every extreme that they name: Every request stands in exactly one serving slot. `page_table`: for each run of 4 serving slots starting at a multiple of 4, the pages listed for their requests come exactly 4 from each of the 16 blocks of 32 pages of page_pool. `routes`: within each aligned block of 16 rows no expert is named by more than 10 rows.
All inputs are finite; a program needn't handle non-finite values.
Results may differ from the reference program's by a relative error of at most 0.0054.
Values may be sent and summed in bfloat16 or wider, within the bound.
No kernel may reach another device: no remote copies, remote signals or barrier semaphores. Data moves between devices by JAX's collectives and lax.ppermute only.
A program may use at most 128 MiB of HBM per device.

```python
import math
import jax
import jax.numpy as jnp
import numpy as np
from jax import lax

D = 3584
HEADS = 64
LAT = 576
KV = 512
FFW = 1024
DRAFT = 4
PAGE = 64
PAGES_REQ = 16
REQ_DEV = 4
POOL = 32
PEERS = 16
EXPERTS = 4
TOP = 2
ROWS_DEV = 16
REQUESTS = 64
ROWS = 256
CAP = 10


def serving_order(key):
    return jax.random.permutation(jax.random.fold_in(key, 11), REQUESTS).astype(jnp.int32)


def draw_serving(key, part):
    return serving_order(key)


def draw_page_table(key, part):
    order = serving_order(key)
    key = jax.random.fold_in(key, 2)
    source_key, local_key = jax.random.split(key)
    listed = REQ_DEV * PAGES_REQ
    repeated = jnp.tile(jnp.arange(PEERS, dtype=jnp.int32), listed // PEERS)
    owner_keys = jax.random.split(source_key, PEERS)

    def shuffled(single):
        return jax.random.permutation(single, repeated)
    sources = jax.vmap(shuffled)(owner_keys)
    resident = jax.random.randint(local_key, (PEERS, listed), 0, POOL)
    listing = (sources * POOL + resident).reshape(REQUESTS, PAGES_REQ).astype(jnp.int32)
    return jnp.zeros((REQUESTS, PAGES_REQ), jnp.int32).at[order].set(listing)


def draw_page_pool(key, part):
    key = jax.random.fold_in(key, 3)
    base_key = jax.random.fold_in(key, 0)
    shape = (PEERS * POOL, PAGE, LAT)
    values = jnp.clip(jax.random.normal(base_key, shape, jnp.float32), -4.0, 4.0)
    return values.reshape(PEERS * POOL, PAGE * LAT).astype(jnp.bfloat16)


def draw_queries(key, part):
    key = jax.random.fold_in(key, 4)
    base_key = jax.random.fold_in(key, 0)
    shape = (ROWS, HEADS, LAT)
    values = jnp.clip(jax.random.normal(base_key, shape, jnp.float32), -4.0, 4.0)
    return values.reshape(ROWS, HEADS * LAT).astype(jnp.bfloat16)


def touch_ends(drawn, key, least, top_value):
    index_at = [jax.random.randint(jax.random.fold_in(key, axis), (), 0, length) for axis, length in enumerate(drawn.shape)]
    widest = drawn.shape.index(max(drawn.shape))
    next_to = index_at[:widest] + [(index_at[widest] + 1) % drawn.shape[widest]] + index_at[widest + 1:]
    return drawn.at[tuple(index_at)].set(least).at[tuple(next_to)].set(top_value)


def block_scale(stream_key, shape, shards, smallest, largest):
    def one(dim, shards_of):
        heights = jax.random.uniform(jax.random.fold_in(jax.random.fold_in(stream_key, 6), dim), (shards_of,), jnp.float32, smallest / len(shards), largest / len(shards))
        return jnp.repeat(jnp.exp(heights), shape[dim] // shards_of).reshape((-1,) + (1,) * (len(shape) - dim - 1))

    loudness = one(*shards[0])
    for cut in shards[1:]:
        loudness = loudness * one(*cut)
    return loudness


def assign_block(key, own, number, rows, number_of, top, limit, slope):
    order = jax.random.permutation(key, number_of)
    packed, common = load_shares(number_of, rows * top, limit, slope, True), load_shares(number_of, rows * top, limit, slope, False)
    places = jnp.arange(number_of)

    def named(tallies, turn):
        used = int((tallies > 0).sum())
        fixed = max(1, used // 4)
        shifted = fixed + (places - fixed + turn * (used - fixed)) % max(1, number_of - fixed)
        return jnp.zeros((number_of,), jnp.int32).at[order[jnp.where(places < fixed, places, shifted)]].set(jnp.asarray(tallies, jnp.int32))

    tallies = jnp.where(number % 4 == 0, named(packed, number // 4), named(common, number - number // 4 - 1))
    mixed = jax.random.permutation(jax.random.fold_in(own, 3), number_of)
    giver, receiver = mixed[0:number_of // 2 * 2:2], mixed[1:number_of // 2 * 2:2]
    room = jnp.minimum(tallies[giver] - 1, limit - tallies[receiver]) // 2
    room = jnp.where((giver == order[0]) | (receiver == order[0]) | (tallies[receiver] == 0), 0, jnp.maximum(room, 0))
    shifted = jax.random.randint(jax.random.fold_in(own, 4), (number_of // 2,), 0, 1 << 20) % (room + 1)
    tallies = tallies.at[giver].add(-shifted).at[receiver].add(shifted)
    labels = jnp.searchsorted(jnp.cumsum(tallies), jnp.arange(rows * top), side="right").astype(jnp.int32)
    grid = labels.reshape(top, rows).T
    grid = grid[jax.random.permutation(jax.random.fold_in(own, 1), rows)]
    turn = jax.random.randint(jax.random.fold_in(own, 2), (rows, 1), 0, top)
    return jnp.take_along_axis(grid, (jnp.arange(top)[None, :] + turn) % top, axis=1)


def load_shares(number_of, total, bound, slope, full):
    portions = [(1 << 20) // math.isqrt(rank ** slope) + 1 for rank in range(1, number_of + 1)]
    largest = bound if full else min(bound, max(-(-total // number_of), total * portions[0] // sum(portions)))
    least = 1 if total - largest >= number_of - 1 else 0
    counts, surplus = [largest] + [least] * (number_of - 1), total - largest - least * (number_of - 1)
    while surplus > 0:
        movable = [i for i in range(1, number_of) if counts[i] < largest] or [i for i in range(1, number_of) if counts[i] < bound]
        pool, left = sum([portions[i] for i in movable]), surplus
        for i in movable:
            more = min(bound - counts[i], max(1, left * portions[i] // pool), surplus)
            counts[i] = counts[i] + more
            surplus = surplus - more
    return np.array(counts)


def bell_draw(stream_key, dims, width, reach, cuts=(), kind=jnp.bfloat16):
    loudness = block_scale(stream_key, dims, cuts, -0.22, 0.18) if cuts else 1.0
    values = jax.random.normal(stream_key, dims, jnp.float32) * width * loudness
    return jnp.minimum(jnp.maximum(values, -reach), reach).astype(kind)


def setup_inputs(seed: int = 0, part: int = 0) -> dict:
    arg_keys = jax.random.split(jax.random.key(seed), 12)
    part_splits = jax.random.split(jax.random.fold_in(arg_keys[11], part), 12)
    queries = draw_queries(jax.random.fold_in(jax.random.fold_in(arg_keys[11], part), 71), part)
    page_pool = draw_page_pool(jax.random.fold_in(jax.random.fold_in(arg_keys[11], part), 71), part)
    page_table = draw_page_table(jax.random.fold_in(jax.random.fold_in(arg_keys[11], part), 71), part)
    serving = draw_serving(jax.random.fold_in(jax.random.fold_in(arg_keys[11], part), 71), part)
    context_len = touch_ends(jax.random.randint(part_splits[4], (REQUESTS,), PAGE * PAGES_REQ // 4, PAGE * PAGES_REQ + 1), jax.random.fold_in(part_splits[4], 1), PAGE * PAGES_REQ // 4, PAGE * PAGES_REQ).astype(jnp.int32)
    residual = bell_draw(part_splits[5], (ROWS, D), 1.0, 6.0, ((0, 16),))
    routes_keys = jax.random.split(jax.random.fold_in(part_splits[6], 1), ROWS // ROWS_DEV)
    routes_turns = jax.random.permutation(jax.random.fold_in(part_splits[6], 3), ROWS // ROWS_DEV)
    routes = jax.vmap(lambda own, number: assign_block(jax.random.fold_in(part_splits[6], 2), own, number, ROWS_DEV, EXPERTS, TOP, CAP, 2))(routes_keys, routes_turns).reshape((ROWS, TOP))
    route_scores = jnp.clip(jnp.exp(math.log(1.0) - 2.3025851 * jax.random.uniform(part_splits[7], (ROWS, TOP), jnp.float32) ** block_scale(part_splits[7], (ROWS, TOP), ((0, 16),), -0.2, 0.2)), 0.1, 1.0)
    w_gate = bell_draw(arg_keys[8], (2 * EXPERTS, D, FFW // 2), D ** -0.5, 0.09375, ((0, 8), (2, 2)))
    w_up = bell_draw(arg_keys[9], (2 * EXPERTS, D, FFW // 2), D ** -0.5, 0.09375, ((0, 8), (2, 2)))
    w_down = bell_draw(arg_keys[10], (2 * EXPERTS, FFW // 2, D), FFW ** -0.5, 0.1875, ((0, 8), (1, 2)))
    return {"queries": queries, "page_pool": page_pool, "page_table": page_table, "serving": serving, "context_len": context_len, "residual": residual, "routes": routes, "route_scores": route_scores, "w_gate": w_gate, "w_up": w_up, "w_down": w_down}


score_scale = 192.0 ** -0.5
masked_score = -1.0e30


def attend(query_rows, context, limits):
    scores = jnp.einsum("thc,kc->thk", query_rows.astype(jnp.float32), context.astype(jnp.float32)) * score_scale
    positions = jnp.arange(context.shape[0], dtype=jnp.int32)
    visible = positions[None, :] <= limits[:, None]
    scores = jnp.where(visible[:, None, :], scores, masked_score)
    highest = jnp.max(scores, axis=-1, keepdims=True)
    exponent = jnp.exp(scores - highest)
    shares = (exponent / jnp.sum(exponent, axis=-1, keepdims=True)).astype(jnp.bfloat16)
    values = context[:, :KV].astype(jnp.float32)
    return jnp.einsum("thk,kc->thc", shares.astype(jnp.float32), values).astype(jnp.bfloat16)


def reference(queries, page_pool, page_table, serving, context_len, residual, routes, route_scores, w_gate, w_up, w_down):
    pages = page_pool.reshape(PEERS * POOL, PAGE, LAT)
    grouped = queries.reshape(REQUESTS, DRAFT, HEADS, LAT)

    def one_request(slot):
        request = serving[slot]
        context = pages[page_table[request]].reshape(PAGES_REQ * PAGE, LAT)
        limits = context_len[request] - DRAFT + jnp.arange(DRAFT, dtype=jnp.int32)
        return attend(grouped[slot], context, limits).reshape(DRAFT, HEADS * KV)

    latent_out = lax.map(one_request, jnp.arange(REQUESTS, dtype=jnp.int32)).reshape(ROWS, HEADS * KV)

    route_weights = route_scores / jnp.sum(route_scores, axis=1, keepdims=True) * 2.5
    half_width = FFW // 2
    gates = w_gate.reshape(EXPERTS, 2, D, half_width)
    uppers = w_up.reshape(EXPERTS, 2, D, half_width)
    downs = w_down.reshape(EXPERTS, 2, half_width, D)

    def one_expert(carry, inputs):
        gate_pair, up_pair, down_pair, expert = inputs
        merged = jnp.zeros((ROWS, D), jnp.float32)
        for half in range(2):
            gate = jnp.dot(residual, gate_pair[half], preferred_element_type=jnp.float32)
            upward = jnp.dot(residual, up_pair[half], preferred_element_type=jnp.float32)
            hidden = (jax.nn.silu(gate) * upward).astype(jnp.bfloat16)
            part_out = jnp.dot(hidden, down_pair[half], preferred_element_type=jnp.float32).astype(jnp.bfloat16)
            merged = merged + part_out.astype(jnp.float32)
        weight = jnp.sum(jnp.where(routes == expert, route_weights, 0.0), axis=1)
        return carry + weight[:, None] * merged, None

    mixed, unused = lax.scan(one_expert, jnp.zeros((ROWS, D), jnp.float32), (gates, uppers, downs, jnp.arange(EXPERTS, dtype=jnp.int32)))
    moe_out = (residual.astype(jnp.float32) + mixed).astype(jnp.bfloat16)
    return latent_out, moe_out
```

```python
import functools

import jax
import jax.numpy as jnp
from jax import lax
from jax.experimental import pallas as pl
from jax.experimental.pallas import tpu as pltpu
from jax.sharding import PartitionSpec as P

HEADS = 64
LAT = 576
KV = 512
DRAFT = 4
HALF = 640
SHIFT = HALF - LAT

score_scale = 192.0 ** (-0.5)
masked_score = -1e30


def stage_body(index_ref, pool_ref, out_ref, pages, sems):
    pages[...] = pool_ref[...].reshape(pages.shape)

    def copy(slot):
        return pltpu.make_async_copy(pages.at[index_ref[slot]], out_ref.at[slot], sems.at[slot])

    def begin(slot, carry):
        copy(slot).start()
        return carry

    def finish(slot, carry):
        copy(slot).wait()
        return carry

    lax.fori_loop(0, out_ref.shape[0], begin, 0)
    lax.fori_loop(0, out_ref.shape[0], finish, 0)


def stage_pages(index, pool):
    pairs = pool.shape[1] // (2 * LAT)
    slots = index.shape[0]
    return pl.pallas_call(
        stage_body,
        out_shape=jax.ShapeDtypeStruct((slots, pairs, 2 * LAT), pool.dtype),
        in_specs=[
            pl.BlockSpec(memory_space=pltpu.SMEM),
            pl.BlockSpec(memory_space=pltpu.VMEM),
        ],
        out_specs=pl.BlockSpec(memory_space=pl.ANY),
        scratch_shapes=[
            pltpu.VMEM((pool.shape[0], pairs, 2 * LAT), pool.dtype),
            pltpu.SemaphoreType.DMA((slots,)),
        ],
        compiler_params=pltpu.CompilerParams(vmem_limit_bytes=32 << 20),
        name="stage_pages",
    )(index, pool)


def attend_body(place_ref, limit_ref, low_ref, high_ref, pages_ref, out_ref, context, held, sems):
    requests, each, pairs, width = context.shape
    rows = low_ref.shape[1]

    def copy(r, i):
        return pltpu.make_async_copy(
            pages_ref.at[place_ref[r * each + i]], context.at[r, i], sems.at[r, i]
        )

    for r in range(requests):

        def begin(i, carry, r=r):
            copy(r, i).start()
            return carry

        lax.fori_loop(0, each, begin, 0)

    columns = each * pairs
    position = 2 * lax.broadcasted_iota(jnp.int32, (rows, columns), 1)
    draft = lax.broadcasted_iota(jnp.int32, (rows, columns), 0) % DRAFT
    early = position - draft
    contract = (((1,), (1,)), ((), ()))
    for r in range(requests):

        def finish(i, carry, r=r):
            copy(r, i).wait()
            return carry

        lax.fori_loop(0, each, finish, 0)
        block = context[r].reshape(columns, width)
        even = lax.dot_general(
            low_ref[r], block[:, :HALF], contract, preferred_element_type=jnp.float32
        )
        odd = lax.dot_general(
            high_ref[r], block[:, width - HALF :], contract, preferred_element_type=jnp.float32
        )
        limit = limit_ref[r]
        even = jnp.where(early <= limit, even * score_scale, masked_score)
        odd = jnp.where(early <= limit - 1, odd * score_scale, masked_score)
        highest = jnp.maximum(
            jnp.max(even, axis=-1, keepdims=True), jnp.max(odd, axis=-1, keepdims=True)
        )
        even = jnp.exp(even - highest)
        odd = jnp.exp(odd - highest)
        total = jnp.sum(even, axis=-1, keepdims=True) + jnp.sum(odd, axis=-1, keepdims=True)
        even = (even / total).astype(jnp.bfloat16)
        odd = (odd / total).astype(jnp.bfloat16)
        latent = jnp.dot(even, block[:, :KV], preferred_element_type=jnp.float32)
        other = jnp.dot(odd, block[:, width - HALF :], preferred_element_type=jnp.float32)
        latent = latent + other[:, SHIFT : SHIFT + KV]
        for h in range(rows // DRAFT):
            held[r * DRAFT : (r + 1) * DRAFT, h * KV : (h + 1) * KV] = latent[
                h * DRAFT : (h + 1) * DRAFT, :
            ]
    out_ref[...] = held[...].astype(out_ref.dtype)


def attend(place, limits, low, high, pages, each):
    requests, rows, _ = low.shape
    _, pairs, width = pages.shape
    out = (requests * DRAFT, (rows // DRAFT) * KV)
    return pl.pallas_call(
        attend_body,
        out_shape=jax.ShapeDtypeStruct(out, jnp.bfloat16),
        in_specs=[
            pl.BlockSpec(memory_space=pltpu.SMEM),
            pl.BlockSpec(memory_space=pltpu.SMEM),
            pl.BlockSpec(memory_space=pltpu.VMEM),
            pl.BlockSpec(memory_space=pltpu.VMEM),
            pl.BlockSpec(memory_space=pl.ANY),
        ],
        out_specs=pl.BlockSpec(memory_space=pltpu.VMEM),
        scratch_shapes=[
            pltpu.VMEM((requests, each, pairs, width), pages.dtype),
            pltpu.VMEM(out, jnp.float32),
            pltpu.SemaphoreType.DMA((requests, each)),
        ],
        compiler_params=pltpu.CompilerParams(vmem_limit_bytes=48 << 20),
        name="attend_pages",
    )(place, limits, low, high, pages)


def local(
    queries,
    page_pool,
    page_table,
    serving,
    context_len,
    residual,
    routes,
    route_scores,
    w_gate,
    w_up,
    w_down,
):
    group = ("ep", "sub")
    peers = lax.axis_size(group)
    device = lax.axis_index(group)
    rows_dev, width = residual.shape
    requests_dev = rows_dev // DRAFT
    pages_each = page_table.shape[1]
    pool_pages = page_pool.shape[0]
    listed = requests_dev * pages_each
    fetched = listed // peers
    n_requests = serving.shape[0]

    slots = jnp.arange(n_requests, dtype=jnp.int32)
    named = serving[:, None] == slots[None, :]
    listing = jnp.sum(jnp.where(named[:, :, None], page_table[None], 0), axis=1).reshape(
        peers, listed
    )
    owners = listing // pool_pages
    mine = owners == device
    position = jnp.arange(listed, dtype=jnp.int32)
    earlier = (position[:, None] < position[None, :]).astype(jnp.bfloat16)
    rank = jnp.dot(mine.astype(jnp.bfloat16), earlier, preferred_element_type=jnp.float32).astype(
        jnp.int32
    )
    nth = jnp.arange(fetched, dtype=jnp.int32)
    taken = mine[:, None, :] & (rank[:, None, :] == nth[None, :, None])
    resident = jnp.sum(jnp.where(taken, listing[:, None, :] - device * pool_pages, 0), axis=2)
    outgoing = stage_pages(resident.reshape(-1), page_pool)
    pairs = outgoing.shape[1]
    arrived = lax.all_to_all(
        outgoing.reshape(peers, fetched, pairs, 2 * LAT), group, split_axis=0, concat_axis=0, tiled=True
    )

    n_ep = lax.axis_size("ep")
    experts = n_ep // 2
    scaled = route_scores / jnp.sum(route_scores, axis=1, keepdims=True) * 2.5
    labels = jnp.arange(experts, dtype=jnp.int32)
    weights = jnp.sum(
        jnp.where(routes[:, :, None] == labels[None, None, :], scaled[:, :, None], 0.0), axis=1
    )
    coarse = lax.reduce_precision(weights, 8, 7)
    rest = weights - coarse
    middle = lax.reduce_precision(rest, 8, 7)
    fine = lax.reduce_precision(rest - middle, 8, 7)
    side = jnp.concatenate([coarse, middle, fine], axis=1).astype(jnp.bfloat16)
    side = jnp.pad(side, ((0, 0), (0, -side.shape[1] % 128)))
    everyone = lax.all_gather(
        jnp.concatenate([residual, side], axis=1), group, axis=0, tiled=True
    )
    rows = everyone[:, :width]
    parts = everyone[:, width : width + 3 * experts].astype(jnp.float32)
    expert = lax.axis_index("ep") // 2
    own = (jnp.arange(3 * experts, dtype=jnp.int32) % experts) == expert
    weight = jnp.sum(jnp.where(own[None, :], parts, 0.0), axis=1, keepdims=True)
    gate = jnp.dot(rows, w_gate[0], preferred_element_type=jnp.float32)
    upward = jnp.dot(rows, w_up[0], preferred_element_type=jnp.float32)
    hidden = (jax.nn.silu(gate) * upward).astype(jnp.bfloat16)
    partial_out = jnp.dot(hidden, w_down[0], preferred_element_type=jnp.float32) * weight
    mixed = lax.psum_scatter(partial_out, group, scatter_dimension=0, tiled=True)
    moe_out = (residual.astype(jnp.float32) + mixed).astype(jnp.bfloat16)

    own_list = lax.dynamic_index_in_dim(owners, device, 0, keepdims=False)
    same = (own_list[:, None] == own_list[None, :]) & (position[None, :] < position[:, None])
    place = own_list * fetched + jnp.sum(same.astype(jnp.int32), axis=1)
    served = lax.dynamic_slice_in_dim(serving, device * requests_dev, requests_dev)
    limits = jnp.sum(
        jnp.where(served[:, None] == slots[None, :], context_len[None, :], 0), axis=1
    ) - DRAFT
    heads = queries.reshape(requests_dev, DRAFT, HEADS, LAT).transpose(0, 2, 1, 3)
    heads = heads.reshape(requests_dev, HEADS * DRAFT, LAT)
    low = jnp.pad(heads, ((0, 0), (0, 0), (0, SHIFT)))
    high = jnp.pad(heads, ((0, 0), (0, 0), (SHIFT, 0)))
    latent_out = attend(
        place, limits, low, high, arrived.reshape(listed, pairs, 2 * LAT), pages_each
    )
    return (latent_out, moe_out)


def solution(mesh):
    placed = (
        P(("rep", "ep", "sub"), None),
        P(("rep", "ep", "sub"), None),
        P("rep", None),
        P("rep"),
        P("rep"),
        P(("rep", "ep", "sub"), None),
        P(("rep", "ep", "sub"), None),
        P(("rep", "ep", "sub"), None),
        P("ep", None, "sub"),
        P("ep", None, "sub"),
        P("ep", "sub", None),
    )
    return jax.shard_map(
        local,
        mesh=mesh,
        in_specs=placed,
        out_specs=(P(("rep", "ep", "sub"), None), P(("rep", "ep", "sub"), None)),
        check_vma=False,
    )
```

```python
import functools

import jax
import jax.numpy as jnp
from jax import lax
from jax.experimental import pallas as pl
from jax.experimental.pallas import tpu as pltpu
from jax.sharding import PartitionSpec as P

HEADS = 64
LAT = 576
KV = 512
DRAFT = 4
HALF = 640
SHIFT = HALF - LAT

score_scale = 192.0 ** (-0.5)
masked_score = -1e30


def ones_where(condition):
    return jnp.where(condition, 1.0, 0.0).astype(jnp.bfloat16)


def count(left, right):
    return jnp.dot(left, right, preferred_element_type=jnp.float32)


def stage_body(
    peers, device_ref, table_ref, serving_ref, pool_ref, out_ref, pool, pages, order, index, *sems
):
    pool_sem, order_sem, page_sems = sems
    fetch = pltpu.make_async_copy(pool_ref, pool, pool_sem)
    fetch.start()
    each, slots = table_ref.shape
    span = slots // peers
    fetched = out_ref.shape[0] // peers
    held = jnp.full((each, slots), pool.shape[0], jnp.int32)
    table = table_ref[...]
    named = ones_where(lax.broadcasted_iota(jnp.int32, (slots, slots), 0) == serving_ref[...])
    owner = count(lax.div(table, held).astype(jnp.float32).astype(jnp.bfloat16), named)
    place = count(lax.rem(table, held).astype(jnp.float32).astype(jnp.bfloat16), named)
    mine = owner == device_ref[0].astype(jnp.float32)
    flags = ones_where(mine)
    above = lax.broadcasted_iota(jnp.int32, (each, each), 1) < lax.broadcasted_iota(
        jnp.int32, (each, each), 0
    )
    first = lax.broadcasted_iota(jnp.int32, (slots, slots), 0)
    second = lax.broadcasted_iota(jnp.int32, (slots, slots), 1)
    spans = jnp.full((slots, slots), span, jnp.int32)
    before = (lax.div(first, spans) == lax.div(second, spans)) & (first < second)
    whole = jnp.ones((each, each), jnp.bfloat16)
    rank = count(ones_where(above), flags) + count(
        count(whole, flags).astype(jnp.bfloat16), ones_where(before)
    )
    serves = ones_where(
        lax.div(
            lax.broadcasted_iota(jnp.int32, (slots, peers), 0),
            jnp.full((slots, peers), span, jnp.int32),
        )
        == lax.broadcasted_iota(jnp.int32, (slots, peers), 1)
    )
    for k in range(fetched):
        chosen = jnp.where(mine & (rank == k), place, 0.0).astype(jnp.bfloat16)
        column = count(count(whole, chosen).astype(jnp.bfloat16), serves)
        order[k : k + 1, :peers] = column[:1].astype(jnp.int32)
    listing = pltpu.make_async_copy(order, index, order_sem)
    listing.start()
    fetch.wait()
    pages[...] = pool[...].reshape(pages.shape)
    listing.wait()

    def copy(p, k):
        slot = p * fetched + k
        return pltpu.make_async_copy(pages.at[index[k, p]], out_ref.at[slot], page_sems.at[slot])

    def begin(p, carry):
        for k in range(fetched):
            copy(p, k).start()
        return carry

    def finish(p, carry):
        for k in range(fetched):
            copy(p, k).wait()
        return carry

    lax.fori_loop(0, peers, begin, 0)
    lax.fori_loop(0, peers, finish, 0)


def stage_pages(device, table, serving, pool, peers, slots):
    pairs = pool.shape[1] // (2 * LAT)
    fetched = slots // peers
    listing = (fetched + -fetched % 8, peers + -peers % 128)
    return pl.pallas_call(
        functools.partial(stage_body, peers),
        out_shape=jax.ShapeDtypeStruct((slots, pairs, 2 * LAT), pool.dtype),
        in_specs=[
            pl.BlockSpec(memory_space=pltpu.SMEM),
            pl.BlockSpec(memory_space=pltpu.VMEM),
            pl.BlockSpec(memory_space=pltpu.VMEM),
            pl.BlockSpec(memory_space=pltpu.HBM),
        ],
        out_specs=pl.BlockSpec(memory_space=pltpu.HBM),
        scratch_shapes=[
            pltpu.VMEM(pool.shape, pool.dtype),
            pltpu.VMEM((pool.shape[0], pairs, 2 * LAT), pool.dtype),
            pltpu.VMEM(listing, jnp.int32),
            pltpu.SMEM(listing, jnp.int32),
            pltpu.SemaphoreType.DMA,
            pltpu.SemaphoreType.DMA,
            pltpu.SemaphoreType.DMA((slots,)),
        ],
        compiler_params=pltpu.CompilerParams(vmem_limit_bytes=32 << 20),
        name="stage_pages",
    )(device, table, serving, pool)


def pack_body(experts, routes_ref, scores_ref, rows_ref, out_ref):
    top, rows = routes_ref.shape
    width = rows_ref.shape[1]
    scores = scores_ref[...]
    scaled = scores / jnp.sum(scores, axis=0, keepdims=True) * 2.5
    labels = lax.broadcasted_iota(jnp.int32, (experts, rows), 0)
    weights = jnp.zeros((experts, rows), jnp.float32)
    for k in range(top):
        weights += jnp.where(labels == routes_ref[k : k + 1, :], scaled[k : k + 1, :], 0.0)
    out_ref[:, :width] = rows_ref[...]
    side = jnp.zeros((rows, out_ref.shape[1] - width), jnp.float32)
    line = lax.broadcasted_iota(jnp.int32, (experts, side.shape[1]), 1)
    entry = lax.broadcasted_iota(jnp.int32, (experts, side.shape[1]), 0)
    for part in range(3):
        piece = weights.astype(jnp.bfloat16)
        weights = weights - piece.astype(jnp.float32)
        side += lax.dot_general(
            piece,
            ones_where(line == entry + part * experts),
            (((0,), (0,)), ((), ())),
            preferred_element_type=jnp.float32,
        )
    out_ref[:, width:] = side.astype(out_ref.dtype)


def pack_rows(routes, scores, rows, experts):
    side = 3 * experts
    width = rows.shape[1] + side + -side % 128
    return pl.pallas_call(
        functools.partial(pack_body, experts),
        out_shape=jax.ShapeDtypeStruct((rows.shape[0], width), rows.dtype),
        name="pack_rows",
    )(routes, scores, rows)


def exchange(block, group, bit):
    peers = lax.axis_size(group)
    return lax.ppermute(block, group, [(d, d ^ bit) for d in range(peers)])


def spread(block, group):
    bit = lax.axis_size(group) // 2
    while bit:
        block = jnp.concatenate([block, exchange(block, group, bit)], axis=0)
        bit //= 2
    return block


def collect(total, group):
    bit = 1
    while bit < lax.axis_size(group):
        half = total.shape[0] // 2
        sent = exchange(total[half:].astype(jnp.bfloat16), group, bit)
        total = total[:half] + sent.astype(jnp.float32)
        bit *= 2
    return total


def attend_body(place_ref, limit_ref, low_ref, high_ref, pages_ref, out_ref, context, held, sems):
    requests, each, pairs, width = context.shape
    rows = low_ref.shape[1]

    def copy(r, i):
        return pltpu.make_async_copy(
            pages_ref.at[place_ref[r * each + i]], context.at[r, i], sems.at[r, i]
        )

    for r in range(requests):

        def begin(i, carry, r=r):
            copy(r, i).start()
            return carry

        lax.fori_loop(0, each, begin, 0)

    columns = each * pairs
    position = 2 * lax.broadcasted_iota(jnp.int32, (rows, columns), 1)
    draft = lax.broadcasted_iota(jnp.int32, (rows, columns), 0) % DRAFT
    early = position - draft
    contract = (((1,), (1,)), ((), ()))
    for r in range(requests):

        def finish(i, carry, r=r):
            copy(r, i).wait()
            return carry

        lax.fori_loop(0, each, finish, 0)
        block = context[r].reshape(columns, width)
        even = lax.dot_general(
            low_ref[r], block[:, :HALF], contract, preferred_element_type=jnp.float32
        )
        odd = lax.dot_general(
            high_ref[r], block[:, width - HALF :], contract, preferred_element_type=jnp.float32
        )
        limit = limit_ref[r]
        even = jnp.where(early <= limit, even * score_scale, masked_score)
        odd = jnp.where(early <= limit - 1, odd * score_scale, masked_score)
        highest = jnp.maximum(
            jnp.max(even, axis=-1, keepdims=True), jnp.max(odd, axis=-1, keepdims=True)
        )
        even = jnp.exp(even - highest)
        odd = jnp.exp(odd - highest)
        total = jnp.sum(even, axis=-1, keepdims=True) + jnp.sum(odd, axis=-1, keepdims=True)
        even = (even / total).astype(jnp.bfloat16)
        odd = (odd / total).astype(jnp.bfloat16)
        latent = jnp.dot(even, block[:, :KV], preferred_element_type=jnp.float32)
        other = jnp.dot(odd, block[:, width - HALF :], preferred_element_type=jnp.float32)
        latent = latent + other[:, SHIFT : SHIFT + KV]
        for h in range(rows // DRAFT):
            held[r * DRAFT : (r + 1) * DRAFT, h * KV : (h + 1) * KV] = latent[
                h * DRAFT : (h + 1) * DRAFT, :
            ]
    out_ref[...] = held[...].astype(out_ref.dtype)


def attend(place, limits, low, high, pages, each):
    requests, rows, _ = low.shape
    _, pairs, width = pages.shape
    out = (requests * DRAFT, (rows // DRAFT) * KV)
    return pl.pallas_call(
        attend_body,
        out_shape=jax.ShapeDtypeStruct(out, jnp.bfloat16),
        in_specs=[
            pl.BlockSpec(memory_space=pltpu.SMEM),
            pl.BlockSpec(memory_space=pltpu.SMEM),
            pl.BlockSpec(memory_space=pltpu.VMEM),
            pl.BlockSpec(memory_space=pltpu.VMEM),
            pl.BlockSpec(memory_space=pltpu.HBM),
        ],
        out_specs=pl.BlockSpec(memory_space=pltpu.VMEM),
        scratch_shapes=[
            pltpu.VMEM((requests, each, pairs, width), pages.dtype),
            pltpu.VMEM(out, jnp.float32),
            pltpu.SemaphoreType.DMA((requests, each)),
        ],
        compiler_params=pltpu.CompilerParams(vmem_limit_bytes=48 << 20),
        name="attend_pages",
    )(place, limits, low, high, pages)


def local(
    queries,
    page_pool,
    page_table,
    serving,
    context_len,
    residual,
    routes,
    route_scores,
    w_gate,
    w_up,
    w_down,
):
    group = ("ep", "sub")
    peers = lax.axis_size(group)
    device = lax.axis_index(group)
    rows_dev, width = residual.shape
    requests_dev = rows_dev // DRAFT
    pages_each = page_table.shape[1]
    pool_pages = page_pool.shape[0]
    listed = requests_dev * pages_each
    fetched = listed // peers
    n_requests = serving.shape[0]

    n_ep = lax.axis_size("ep")
    experts = n_ep // 2
    everyone = spread(pack_rows(routes.T, route_scores.T, residual, experts), group)

    outgoing = stage_pages(
        device.reshape(1), page_table.T, serving.reshape(1, -1), page_pool, peers, listed
    )
    pairs = outgoing.shape[1]
    arrived = lax.all_to_all(
        outgoing.reshape(peers, fetched, pairs, 2 * LAT), group, split_axis=0, concat_axis=0, tiled=True
    )

    rows = everyone[:, :width]
    parts = everyone[:, width : width + 3 * experts].astype(jnp.float32)
    expert = lax.axis_index("ep") // 2
    own = (jnp.arange(3 * experts, dtype=jnp.int32) % experts) == expert
    weight = jnp.sum(jnp.where(own[None, :], parts, 0.0), axis=1, keepdims=True)
    gate = jnp.dot(rows, w_gate[0], preferred_element_type=jnp.float32)
    upward = jnp.dot(rows, w_up[0], preferred_element_type=jnp.float32)
    hidden = (jax.nn.silu(gate) * upward).astype(jnp.bfloat16)
    partial_out = jnp.dot(hidden, w_down[0], preferred_element_type=jnp.float32) * weight
    mixed = collect(partial_out, group)
    moe_out = (residual.astype(jnp.float32) + mixed).astype(jnp.bfloat16)

    served = lax.dynamic_slice_in_dim(serving, device * requests_dev, requests_dev)
    slots = jnp.arange(n_requests, dtype=jnp.int32)
    chosen = served[:, None] == slots[None, :]
    own_list = jnp.sum(jnp.where(chosen[:, :, None], page_table[None], 0), axis=1)
    own_list = own_list.reshape(-1) // pool_pages
    position = jnp.arange(listed, dtype=jnp.int32)
    same = (own_list[:, None] == own_list[None, :]) & (position[None, :] < position[:, None])
    place = own_list * fetched + jnp.sum(same.astype(jnp.int32), axis=1)
    limits = jnp.sum(jnp.where(chosen, context_len[None, :], 0), axis=1) - DRAFT
    heads = queries.reshape(requests_dev, DRAFT, HEADS, LAT).transpose(0, 2, 1, 3)
    heads = heads.reshape(requests_dev, HEADS * DRAFT, LAT)
    low = jnp.pad(heads, ((0, 0), (0, 0), (0, SHIFT)))
    high = jnp.pad(heads, ((0, 0), (0, 0), (SHIFT, 0)))
    latent_out = attend(
        place, limits, low, high, arrived.reshape(listed, pairs, 2 * LAT), pages_each
    )
    return (latent_out, moe_out)


def solution(mesh):
    placed = (
        P(("rep", "ep", "sub"), None),
        P(("rep", "ep", "sub"), None),
        P("rep", None),
        P("rep"),
        P("rep"),
        P(("rep", "ep", "sub"), None),
        P(("rep", "ep", "sub"), None),
        P(("rep", "ep", "sub"), None),
        P("ep", None, "sub"),
        P("ep", None, "sub"),
        P("ep", "sub", None),
    )
    return jax.shard_map(
        local,
        mesh=mesh,
        in_specs=placed,
        out_specs=(P(("rep", "ep", "sub"), None), P(("rep", "ep", "sub"), None)),
        check_vma=False,
    )
```

```python
import functools

import jax
import jax.numpy as jnp
from jax import lax
from jax.experimental import pallas as pl
from jax.experimental.pallas import tpu as pltpu
from jax.sharding import PartitionSpec as P

HEADS = 64
LAT = 576
KV = 512
DRAFT = 4
HALF = 640
SHIFT = HALF - LAT

score_scale = 192.0 ** (-0.5)
masked_score = -1e30


def ones_where(condition):
    return jnp.where(condition, 1.0, 0.0).astype(jnp.bfloat16)


def count(left, right):
    return jnp.dot(left, right, preferred_element_type=jnp.float32)


def stage_body(
    peers, device_ref, table_ref, serving_ref, pool_ref, out_ref, pool, pages, order, index, *sems
):
    pool_sem, order_sem, page_sems = sems
    fetch = pltpu.make_async_copy(pool_ref, pool, pool_sem)
    fetch.start()
    each, slots = table_ref.shape
    span = slots // peers
    fetched = out_ref.shape[0] // peers
    held = jnp.full((each, slots), pool.shape[0], jnp.int32)
    table = table_ref[...]
    named = ones_where(lax.broadcasted_iota(jnp.int32, (slots, slots), 0) == serving_ref[...])
    owner = count(lax.div(table, held).astype(jnp.float32).astype(jnp.bfloat16), named)
    place = count(lax.rem(table, held).astype(jnp.float32).astype(jnp.bfloat16), named)
    mine = owner == device_ref[0].astype(jnp.float32)
    flags = ones_where(mine)
    above = lax.broadcasted_iota(jnp.int32, (each, each), 1) < lax.broadcasted_iota(
        jnp.int32, (each, each), 0
    )
    first = lax.broadcasted_iota(jnp.int32, (slots, slots), 0)
    second = lax.broadcasted_iota(jnp.int32, (slots, slots), 1)
    spans = jnp.full((slots, slots), span, jnp.int32)
    before = (lax.div(first, spans) == lax.div(second, spans)) & (first < second)
    whole = jnp.ones((each, each), jnp.bfloat16)
    rank = count(ones_where(above), flags) + count(
        count(whole, flags).astype(jnp.bfloat16), ones_where(before)
    )
    serves = ones_where(
        lax.div(
            lax.broadcasted_iota(jnp.int32, (slots, peers), 0),
            jnp.full((slots, peers), span, jnp.int32),
        )
        == lax.broadcasted_iota(jnp.int32, (slots, peers), 1)
    )
    for k in range(fetched):
        chosen = jnp.where(mine & (rank == k), place, 0.0).astype(jnp.bfloat16)
        column = count(count(whole, chosen).astype(jnp.bfloat16), serves)
        order[k : k + 1, :peers] = column[:1].astype(jnp.int32)
    listing = pltpu.make_async_copy(order, index, order_sem)
    listing.start()
    fetch.wait()
    pages[...] = pool[...].reshape(pages.shape)
    listing.wait()

    def copy(p, k):
        slot = p * fetched + k
        return pltpu.make_async_copy(pages.at[index[k, p]], out_ref.at[slot], page_sems.at[slot])

    def begin(p, carry):
        for k in range(fetched):
            copy(p, k).start()
        return carry

    def finish(p, carry):
        for k in range(fetched):
            copy(p, k).wait()
        return carry

    lax.fori_loop(0, peers, begin, 0)
    lax.fori_loop(0, peers, finish, 0)


def stage_pages(device, table, serving, pool, peers, slots):
    pairs = pool.shape[1] // (2 * LAT)
    fetched = slots // peers
    listing = (fetched + -fetched % 8, peers + -peers % 128)
    return pl.pallas_call(
        functools.partial(stage_body, peers),
        out_shape=jax.ShapeDtypeStruct((slots, pairs, 2 * LAT), pool.dtype),
        in_specs=[
            pl.BlockSpec(memory_space=pltpu.SMEM),
            pl.BlockSpec(memory_space=pltpu.VMEM),
            pl.BlockSpec(memory_space=pltpu.VMEM),
            pl.BlockSpec(memory_space=pltpu.HBM),
        ],
        out_specs=pl.BlockSpec(memory_space=pltpu.HBM),
        scratch_shapes=[
            pltpu.VMEM(pool.shape, pool.dtype),
            pltpu.VMEM((pool.shape[0], pairs, 2 * LAT), pool.dtype),
            pltpu.VMEM(listing, jnp.int32),
            pltpu.SMEM(listing, jnp.int32),
            pltpu.SemaphoreType.DMA,
            pltpu.SemaphoreType.DMA,
            pltpu.SemaphoreType.DMA((slots,)),
        ],
        compiler_params=pltpu.CompilerParams(vmem_limit_bytes=56 << 20),
        name="stage_pages",
    )(device, table, serving, pool)


def pack_body(experts, routes_ref, scores_ref, rows_ref, out_ref):
    top, rows = routes_ref.shape
    width = rows_ref.shape[1]
    scores = scores_ref[...]
    scaled = scores / jnp.sum(scores, axis=0, keepdims=True) * 2.5
    labels = lax.broadcasted_iota(jnp.int32, (experts, rows), 0)
    weights = jnp.zeros((experts, rows), jnp.float32)
    for k in range(top):
        weights += jnp.where(labels == routes_ref[k : k + 1, :], scaled[k : k + 1, :], 0.0)
    out_ref[:, :width] = rows_ref[...]
    side = jnp.zeros((rows, out_ref.shape[1] - width), jnp.float32)
    line = lax.broadcasted_iota(jnp.int32, (experts, side.shape[1]), 1)
    entry = lax.broadcasted_iota(jnp.int32, (experts, side.shape[1]), 0)
    for part in range(3):
        piece = weights.astype(jnp.bfloat16)
        weights = weights - piece.astype(jnp.float32)
        side += lax.dot_general(
            piece,
            ones_where(line == entry + part * experts),
            (((0,), (0,)), ((), ())),
            preferred_element_type=jnp.float32,
        )
    out_ref[:, width:] = side.astype(out_ref.dtype)


def pack_rows(routes, scores, rows, experts):
    side = 3 * experts
    width = rows.shape[1] + side + -side % 128
    return pl.pallas_call(
        functools.partial(pack_body, experts),
        out_shape=jax.ShapeDtypeStruct((rows.shape[0], width), rows.dtype),
        name="pack_rows",
    )(routes, scores, rows)


def exchange(block, group, bit):
    peers = lax.axis_size(group)
    return lax.ppermute(block, group, [(d, d ^ bit) for d in range(peers)])


def spread(block, group, bit):
    while bit:
        block = jnp.concatenate([block, exchange(block, group, bit)], axis=0)
        bit //= 2
    return block


def collect(total, group):
    bit = 1
    while True:
        half = total.shape[0] // 2
        sent = exchange(total[half:].astype(jnp.bfloat16), group, bit)
        bit *= 2
        if bit == lax.axis_size(group):
            return total[:half], sent
        total = total[:half] + sent.astype(jnp.float32)


def attend_body(
    place_ref, limit_ref, low_hbm, high_hbm, pages_ref, out_ref, context, held, low_ref, high_ref, *sems
):
    requests, each, pairs, width = context.shape
    rows = low_ref.shape[1]
    page_sems, low_sems, high_sems = sems

    def copy(r, i):
        return pltpu.make_async_copy(
            pages_ref.at[place_ref[r * each + i]], context.at[r, i], page_sems.at[r, i]
        )

    def copy_queries(r):
        return (
            pltpu.make_async_copy(low_hbm.at[r], low_ref.at[r], low_sems.at[r]),
            pltpu.make_async_copy(high_hbm.at[r], high_ref.at[r], high_sems.at[r]),
        )

    for r in range(requests):
        for query_copy in copy_queries(r):
            query_copy.start()

        def begin(i, carry, r=r):
            copy(r, i).start()
            return carry

        lax.fori_loop(0, each, begin, 0)

    columns = each * pairs
    position = 2 * lax.broadcasted_iota(jnp.int32, (rows, columns), 1)
    draft = lax.broadcasted_iota(jnp.int32, (rows, columns), 0) % DRAFT
    early = position - draft
    contract = (((1,), (1,)), ((), ()))
    for r in range(requests):

        def finish(i, carry, r=r):
            copy(r, i).wait()
            return carry

        for query_copy in copy_queries(r):
            query_copy.wait()
        lax.fori_loop(0, each, finish, 0)
        block = context[r].reshape(columns, width)
        even = lax.dot_general(
            low_ref[r], block[:, :HALF], contract, preferred_element_type=jnp.float32
        )
        odd = lax.dot_general(
            high_ref[r], block[:, width - HALF :], contract, preferred_element_type=jnp.float32
        )
        limit = limit_ref[r]
        even = jnp.where(early <= limit, even * score_scale, masked_score)
        odd = jnp.where(early <= limit - 1, odd * score_scale, masked_score)
        highest = jnp.maximum(
            jnp.max(even, axis=-1, keepdims=True), jnp.max(odd, axis=-1, keepdims=True)
        )
        even = jnp.exp(even - highest)
        odd = jnp.exp(odd - highest)
        total = jnp.sum(even, axis=-1, keepdims=True) + jnp.sum(odd, axis=-1, keepdims=True)
        even = (even / total).astype(jnp.bfloat16)
        odd = (odd / total).astype(jnp.bfloat16)
        latent = jnp.dot(even, block[:, :KV], preferred_element_type=jnp.float32)
        other = jnp.dot(odd, block[:, width - HALF :], preferred_element_type=jnp.float32)
        latent = latent + other[:, SHIFT : SHIFT + KV]
        for h in range(rows // DRAFT):
            held[r * DRAFT : (r + 1) * DRAFT, h * KV : (h + 1) * KV] = latent[
                h * DRAFT : (h + 1) * DRAFT, :
            ]
    out_ref[...] = held[...].astype(out_ref.dtype)


def attend(place, limits, low, high, pages, each):
    requests, rows, _ = low.shape
    _, pairs, width = pages.shape
    out = (requests * DRAFT, (rows // DRAFT) * KV)
    return pl.pallas_call(
        attend_body,
        out_shape=jax.ShapeDtypeStruct(out, jnp.bfloat16),
        in_specs=[
            pl.BlockSpec(memory_space=pltpu.SMEM),
            pl.BlockSpec(memory_space=pltpu.SMEM),
            pl.BlockSpec(memory_space=pltpu.HBM),
            pl.BlockSpec(memory_space=pltpu.HBM),
            pl.BlockSpec(memory_space=pltpu.HBM),
        ],
        out_specs=pl.BlockSpec(memory_space=pltpu.VMEM),
        scratch_shapes=[
            pltpu.VMEM((requests, each, pairs, width), pages.dtype),
            pltpu.VMEM(out, jnp.float32),
            pltpu.VMEM(low.shape, low.dtype),
            pltpu.VMEM(high.shape, high.dtype),
            pltpu.SemaphoreType.DMA((requests, each)),
            pltpu.SemaphoreType.DMA((requests,)),
            pltpu.SemaphoreType.DMA((requests,)),
        ],
        compiler_params=pltpu.CompilerParams(vmem_limit_bytes=56 << 20),
        name="attend_pages",
    )(place, limits, low, high, pages)


def local(
    queries,
    page_pool,
    page_table,
    serving,
    context_len,
    residual,
    routes,
    route_scores,
    w_gate,
    w_up,
    w_down,
):
    group = ("ep", "sub")
    peers = lax.axis_size(group)
    device = lax.axis_index(group)
    rows_dev, width = residual.shape
    requests_dev = rows_dev // DRAFT
    pages_each = page_table.shape[1]
    pool_pages = page_pool.shape[0]
    listed = requests_dev * pages_each
    fetched = listed // peers
    n_requests = serving.shape[0]

    n_ep = lax.axis_size("ep")
    experts = n_ep // 2
    packed = pack_rows(routes.T, route_scores.T, residual, experts)
    far, near = peers // 2, peers // 4
    across = [exchange(packed, group, bit) for bit in (far, near, far | near)]

    outgoing = stage_pages(
        device.reshape(1), page_table.T, serving.reshape(1, -1), page_pool, peers, listed
    )
    packed, across, outgoing = lax.optimization_barrier((packed, across, outgoing))
    pairs = outgoing.shape[1]
    arrived = lax.all_to_all(
        outgoing.reshape(peers, fetched, pairs, 2 * LAT), group, split_axis=0, concat_axis=0, tiled=True
    )

    everyone = spread(jnp.concatenate([packed, *across], axis=0), group, near // 2)
    rows = everyone[:, :width]
    parts = everyone[:, width : width + 3 * experts].astype(jnp.float32)
    expert = lax.axis_index("ep") // 2
    own = (jnp.arange(3 * experts, dtype=jnp.int32) % experts) == expert
    weight = jnp.sum(jnp.where(own[None, :], parts, 0.0), axis=1, keepdims=True)
    gate = jnp.dot(rows, w_gate[0], preferred_element_type=jnp.float32)
    upward = jnp.dot(rows, w_up[0], preferred_element_type=jnp.float32)
    hidden = (jax.nn.silu(gate) * upward).astype(jnp.bfloat16)
    partial_out = jnp.dot(hidden, w_down[0], preferred_element_type=jnp.float32) * weight
    mixed, last = collect(partial_out, group)

    served = lax.dynamic_slice_in_dim(serving, device * requests_dev, requests_dev)
    slots = jnp.arange(n_requests, dtype=jnp.int32)
    chosen = served[:, None] == slots[None, :]
    own_list = jnp.sum(jnp.where(chosen[:, :, None], page_table[None], 0), axis=1)
    own_list = own_list.reshape(-1) // pool_pages
    position = jnp.arange(listed, dtype=jnp.int32)
    same = (own_list[:, None] == own_list[None, :]) & (position[None, :] < position[:, None])
    place = own_list * fetched + jnp.sum(same.astype(jnp.int32), axis=1)
    limits = jnp.sum(jnp.where(chosen, context_len[None, :], 0), axis=1) - DRAFT
    heads = queries.reshape(requests_dev, DRAFT, HEADS, LAT).transpose(0, 2, 1, 3)
    heads = heads.reshape(requests_dev, HEADS * DRAFT, LAT)
    low = jnp.pad(heads, ((0, 0), (0, 0), (0, SHIFT)))
    high = jnp.pad(heads, ((0, 0), (0, 0), (SHIFT, 0)))
    latent_out = attend(
        place, limits, low, high, arrived.reshape(listed, pairs, 2 * LAT), pages_each
    )
    latent_out, last = lax.optimization_barrier((latent_out, last))
    moe_out = (residual.astype(jnp.float32) + mixed + last.astype(jnp.float32)).astype(jnp.bfloat16)
    return (latent_out, moe_out)


def solution(mesh):
    placed = (
        P(("rep", "ep", "sub"), None),
        P(("rep", "ep", "sub"), None),
        P("rep", None),
        P("rep"),
        P("rep"),
        P(("rep", "ep", "sub"), None),
        P(("rep", "ep", "sub"), None),
        P(("rep", "ep", "sub"), None),
        P("ep", None, "sub"),
        P("ep", None, "sub"),
        P("ep", "sub", None),
    )
    return jax.shard_map(
        local,
        mesh=mesh,
        in_specs=placed,
        out_specs=(P(("rep", "ep", "sub"), None), P(("rep", "ep", "sub"), None)),
        check_vma=False,
    )
```

```python
import functools
import math

import jax
import jax.numpy as jnp
from jax import lax
from jax.experimental import pallas as pl
from jax.experimental.pallas import tpu as pltpu
from jax.sharding import PartitionSpec as P

HEADS = 64
LAT = 576
KV = 512
DRAFT = 4
HALF = 640
SHIFT = HALF - LAT

exponent_scale = 192.0 ** (-0.5) * math.log2(math.e)
masked_score = -1e30


def ones_where(condition):
    return jnp.where(condition, 1.0, 0.0).astype(jnp.bfloat16)


def count(left, right):
    return jnp.dot(left, right, preferred_element_type=jnp.float32)


def stage_body(
    peers, device_ref, table_ref, serving_ref, pool_ref, out_ref, pool, pages, order, index, *sems
):
    pool_sem, order_sem, page_sems = sems
    fetch = pltpu.make_async_copy(pool_ref, pool, pool_sem)
    fetch.start()
    each, slots = table_ref.shape
    span = slots // peers
    fetched = out_ref.shape[0] // peers
    held = jnp.full((each, slots), pool.shape[0], jnp.int32)
    table = table_ref[...]
    named = ones_where(lax.broadcasted_iota(jnp.int32, (slots, slots), 0) == serving_ref[...])
    owner = count(lax.div(table, held).astype(jnp.float32).astype(jnp.bfloat16), named)
    place = count(lax.rem(table, held).astype(jnp.float32).astype(jnp.bfloat16), named)
    mine = owner == device_ref[0].astype(jnp.float32)
    flags = ones_where(mine)
    above = lax.broadcasted_iota(jnp.int32, (each, each), 1) < lax.broadcasted_iota(
        jnp.int32, (each, each), 0
    )
    first = lax.broadcasted_iota(jnp.int32, (slots, slots), 0)
    second = lax.broadcasted_iota(jnp.int32, (slots, slots), 1)
    spans = jnp.full((slots, slots), span, jnp.int32)
    before = (lax.div(first, spans) == lax.div(second, spans)) & (first < second)
    whole = jnp.ones((each, each), jnp.bfloat16)
    rank = count(ones_where(above), flags) + count(
        count(whole, flags).astype(jnp.bfloat16), ones_where(before)
    )
    serves = ones_where(
        lax.div(
            lax.broadcasted_iota(jnp.int32, (slots, peers), 0),
            jnp.full((slots, peers), span, jnp.int32),
        )
        == lax.broadcasted_iota(jnp.int32, (slots, peers), 1)
    )
    for k in range(fetched):
        chosen = jnp.where(mine & (rank == k), place, 0.0).astype(jnp.bfloat16)
        column = count(count(whole, chosen).astype(jnp.bfloat16), serves)
        order[k : k + 1, :peers] = column[:1].astype(jnp.int32)
    listing = pltpu.make_async_copy(order, index, order_sem)
    listing.start()
    fetch.wait()
    pages[...] = pool[...].reshape(pages.shape)
    listing.wait()

    def copy(p, k):
        slot = p * fetched + k
        return pltpu.make_async_copy(pages.at[index[k, p]], out_ref.at[slot], page_sems.at[slot])

    def begin(p, carry):
        for k in range(fetched):
            copy(p, k).start()
        return carry

    def finish(p, carry):
        for k in range(fetched):
            copy(p, k).wait()
        return carry

    lax.fori_loop(0, peers, begin, 0)
    lax.fori_loop(0, peers, finish, 0)


def stage_pages(device, table, serving, pool, peers, slots):
    pairs = pool.shape[1] // (2 * LAT)
    fetched = slots // peers
    listing = (fetched + -fetched % 8, peers + -peers % 128)
    return pl.pallas_call(
        functools.partial(stage_body, peers),
        out_shape=jax.ShapeDtypeStruct((slots, pairs, 2 * LAT), pool.dtype),
        in_specs=[
            pl.BlockSpec(memory_space=pltpu.SMEM),
            pl.BlockSpec(memory_space=pltpu.VMEM),
            pl.BlockSpec(memory_space=pltpu.VMEM),
            pl.BlockSpec(memory_space=pltpu.HBM),
        ],
        out_specs=pl.BlockSpec(memory_space=pltpu.HBM),
        scratch_shapes=[
            pltpu.VMEM(pool.shape, pool.dtype),
            pltpu.VMEM((pool.shape[0], pairs, 2 * LAT), pool.dtype),
            pltpu.VMEM(listing, jnp.int32),
            pltpu.SMEM(listing, jnp.int32),
            pltpu.SemaphoreType.DMA,
            pltpu.SemaphoreType.DMA,
            pltpu.SemaphoreType.DMA((slots,)),
        ],
        compiler_params=pltpu.CompilerParams(vmem_limit_bytes=56 << 20),
        name="stage_pages",
    )(device, table, serving, pool)


def pack_body(experts, routes_ref, scores_ref, rows_ref, out_ref):
    top, rows = routes_ref.shape
    width = rows_ref.shape[1]
    scores = scores_ref[...]
    scaled = scores / jnp.sum(scores, axis=0, keepdims=True) * 2.5
    labels = lax.broadcasted_iota(jnp.int32, (experts, rows), 0)
    weights = jnp.zeros((experts, rows), jnp.float32)
    for k in range(top):
        weights += jnp.where(labels == routes_ref[k : k + 1, :], scaled[k : k + 1, :], 0.0)
    out_ref[:, :width] = rows_ref[...]
    side = jnp.zeros((rows, out_ref.shape[1] - width), jnp.float32)
    line = lax.broadcasted_iota(jnp.int32, (experts, side.shape[1]), 1)
    entry = lax.broadcasted_iota(jnp.int32, (experts, side.shape[1]), 0)
    for part in range(3):
        piece = weights.astype(jnp.bfloat16)
        weights = weights - piece.astype(jnp.float32)
        side += lax.dot_general(
            piece,
            ones_where(line == entry + part * experts),
            (((0,), (0,)), ((), ())),
            preferred_element_type=jnp.float32,
        )
    out_ref[:, width:] = side.astype(out_ref.dtype)


def pack_rows(routes, scores, rows, experts):
    side = 3 * experts
    width = rows.shape[1] + side + -side % 128
    return pl.pallas_call(
        functools.partial(pack_body, experts),
        out_shape=jax.ShapeDtypeStruct((rows.shape[0], width), rows.dtype),
        name="pack_rows",
    )(routes, scores, rows)


def exchange(block, group, bit):
    peers = lax.axis_size(group)
    return lax.ppermute(block, group, [(d, d ^ bit) for d in range(peers)])


def expert_body(experts, label_ref, kept_ref, other_ref, *refs):
    gate_hbm, up_hbm, down_hbm, kept_out, other_out, gate_ref, up_ref, down_ref, sems = refs
    copies = [
        pltpu.make_async_copy(gate_hbm, gate_ref, sems.at[0]),
        pltpu.make_async_copy(up_hbm, up_ref, sems.at[1]),
        pltpu.make_async_copy(down_hbm, down_ref, sems.at[2]),
    ]
    for weight_copy in copies:
        weight_copy.start()
    width = gate_ref.shape[0]
    parts = []
    copies[0].wait()
    for rows_ref in (other_ref, kept_ref):
        parts.append(jnp.dot(rows_ref[:, :width], gate_ref[...], preferred_element_type=jnp.float32))
    copies[1].wait()
    hiddens = []
    for rows_ref, gate in zip((other_ref, kept_ref), parts):
        upward = jnp.dot(rows_ref[:, :width], up_ref[...], preferred_element_type=jnp.float32)
        hiddens.append((gate / (1.0 + jnp.exp(-gate)) * upward).astype(jnp.bfloat16))
    copies[2].wait()
    for rows_ref, hidden, out_ref in zip((other_ref, kept_ref), hiddens, (other_out, kept_out)):
        side = rows_ref[:, width:].astype(jnp.float32)
        line = lax.broadcasted_iota(jnp.int32, side.shape, 1)
        mine = (line == label_ref[0]) | (line == label_ref[0] + experts)
        mine = mine | (line == label_ref[0] + 2 * experts)
        weight = jnp.sum(jnp.where(mine, side, 0.0), axis=1, keepdims=True)
        total = jnp.dot(hidden, down_ref[...], preferred_element_type=jnp.float32) * weight
        out_ref[...] = total.astype(out_ref.dtype)


def expert_rows(label, kept, other, gate, up, down, experts):
    return pl.pallas_call(
        functools.partial(expert_body, experts),
        out_shape=(
            jax.ShapeDtypeStruct((kept.shape[0], gate.shape[0]), jnp.float32),
            jax.ShapeDtypeStruct((other.shape[0], gate.shape[0]), jnp.bfloat16),
        ),
        in_specs=[pl.BlockSpec(memory_space=pltpu.SMEM)]
        + [pl.BlockSpec(memory_space=pltpu.VMEM)] * 2
        + [pl.BlockSpec(memory_space=pltpu.HBM)] * 3,
        scratch_shapes=[
            pltpu.VMEM(gate.shape, gate.dtype),
            pltpu.VMEM(up.shape, up.dtype),
            pltpu.VMEM(down.shape, down.dtype),
            pltpu.SemaphoreType.DMA((3,)),
        ],
        compiler_params=pltpu.CompilerParams(vmem_limit_bytes=56 << 20),
        cost_estimate=pl.CostEstimate(flops=0, bytes_accessed=0, transcendentals=0),
        name="expert_rows",
    )(label, kept, other, gate, up, down)


def attend_body(plan_ref, query_ref, pages_ref, out_ref, context, held, sems):
    requests, each, pairs, width = context.shape
    rows = query_ref.shape[1]
    contract = (((1,), (1,)), ((), ()))

    def copy(r, i):
        return pltpu.make_async_copy(
            pages_ref.at[plan_ref[2 * requests + r * each + i]], context.at[r, i], sems.at[r * each + i]
        )

    blank = jnp.zeros((pairs, width), context.dtype)
    for r in range(requests):

        def begin(i, carry, r=r):
            copy(r, i).start()
            return carry

        lax.fori_loop(0, plan_ref[r], begin, 0)
    for r in range(requests):

        def clear(i, carry, r=r):
            context[r, i] = blank
            return carry

        lax.fori_loop(plan_ref[r], each, clear, 0)

    columns = each * pairs
    draft = lax.broadcasted_iota(jnp.int32, (rows, columns), 0) % DRAFT
    early = 2 * lax.broadcasted_iota(jnp.int32, (rows, columns), 1) - draft

    def score(r):
        def finish(i, carry):
            copy(r, i).wait()
            return carry

        lax.fori_loop(0, plan_ref[r], finish, 0)
        block = context[r].reshape(columns, width)
        low = query_ref[r]
        high = pltpu.roll(low.astype(jnp.float32), SHIFT, 1).astype(low.dtype)
        even = lax.dot_general(
            low, block[:, :HALF], contract, preferred_element_type=jnp.float32
        )
        odd = lax.dot_general(
            high, block[:, width - HALF :], contract, preferred_element_type=jnp.float32
        )
        return even, odd

    scored = score(0)
    for r in range(requests):
        even, odd = scored
        if r + 1 < requests:
            scored = score(r + 1)
        limit = plan_ref[requests + r]
        even = jnp.where(early <= limit, even, masked_score)
        odd = jnp.where(early < limit, odd, masked_score)
        highest = jnp.max(jnp.maximum(even, odd), axis=-1, keepdims=True)
        even = jnp.exp2((even - highest) * exponent_scale)
        odd = jnp.exp2((odd - highest) * exponent_scale)
        total = jnp.sum(even + odd, axis=-1, keepdims=True)
        block = context[r].reshape(columns, width)
        latent = jnp.dot(
            even.astype(jnp.bfloat16), block[:, :KV], preferred_element_type=jnp.float32
        )
        other = jnp.dot(
            odd.astype(jnp.bfloat16), block[:, width - HALF :], preferred_element_type=jnp.float32
        )
        latent = (latent + other[:, SHIFT : SHIFT + KV]) * (1.0 / total)
        for h in range(rows // DRAFT):
            held[r * DRAFT : (r + 1) * DRAFT, h * KV : (h + 1) * KV] = latent[
                h * DRAFT : (h + 1) * DRAFT, :
            ]
    out_ref[...] = held[...].astype(out_ref.dtype)


def attend(plan, query, pages, each):
    requests, rows, _ = query.shape
    _, pairs, width = pages.shape
    out = (requests * DRAFT, (rows // DRAFT) * KV)
    return pl.pallas_call(
        attend_body,
        out_shape=jax.ShapeDtypeStruct(out, jnp.bfloat16),
        in_specs=[
            pl.BlockSpec(memory_space=pltpu.SMEM),
            pl.BlockSpec(memory_space=pltpu.VMEM),
            pl.BlockSpec(memory_space=pltpu.HBM),
        ],
        out_specs=pl.BlockSpec(memory_space=pltpu.VMEM),
        scratch_shapes=[
            pltpu.VMEM((requests, each, pairs, width), pages.dtype),
            pltpu.VMEM(out, jnp.float32),
            pltpu.SemaphoreType.DMA((requests * each,)),
        ],
        compiler_params=pltpu.CompilerParams(vmem_limit_bytes=50 << 20),
        name="attend_pages",
    )(plan, query, pages)


def local(
    queries,
    page_pool,
    page_table,
    serving,
    context_len,
    residual,
    routes,
    route_scores,
    w_gate,
    w_up,
    w_down,
):
    group = ("ep", "sub")
    peers = lax.axis_size(group)
    device = lax.axis_index(group)
    rows_dev, width = residual.shape
    requests_dev = rows_dev // DRAFT
    pages_each = page_table.shape[1]
    pool_pages = page_pool.shape[0]
    listed = requests_dev * pages_each
    fetched = listed // peers
    n_requests = serving.shape[0]

    n_ep = lax.axis_size("ep")
    experts = n_ep // 2
    packed = pack_rows(routes.T, route_scores.T, residual, experts)
    far, near = peers // 2, peers // 4
    across = [exchange(packed, group, bit) for bit in (far, near, far | near)]

    outgoing = stage_pages(
        device.reshape(1), page_table.T, serving.reshape(1, -1), page_pool, peers, listed
    )
    packed, across, outgoing = lax.optimization_barrier((packed, across, outgoing))
    pairs = outgoing.shape[1]
    arrived = lax.all_to_all(
        outgoing.reshape(peers, fetched, pairs, 2 * LAT), group, split_axis=0, concat_axis=0, tiled=True
    )

    kept = jnp.concatenate([packed, *across], axis=0)
    bit = near // 2
    while bit > 1:
        kept = jnp.concatenate([kept, exchange(kept, group, bit)], axis=0)
        bit //= 2
    other = exchange(kept, group, 1)
    label = (lax.axis_index("ep") // 2).reshape(1)
    mixed, leaving = expert_rows(label, kept, other, w_gate[0], w_up[0], w_down[0], experts)
    bit = 1
    while True:
        last = exchange(leaving, group, bit)
        bit *= 2
        if bit == peers:
            break
        mixed = mixed + last.astype(jnp.float32)
        half = mixed.shape[0] // 2
        leaving = mixed[half:].astype(jnp.bfloat16)
        mixed = mixed[:half]

    served = lax.dynamic_slice_in_dim(serving, device * requests_dev, requests_dev)
    slots = jnp.arange(n_requests, dtype=jnp.int32)
    chosen = served[:, None] == slots[None, :]
    own_list = jnp.sum(jnp.where(chosen[:, :, None], page_table[None], 0), axis=1)
    own_list = own_list.reshape(-1) // pool_pages
    position = jnp.arange(listed, dtype=jnp.int32)
    same = (own_list[:, None] == own_list[None, :]) & (position[None, :] < position[:, None])
    place = own_list * fetched + jnp.sum(same.astype(jnp.int32), axis=1)
    limits = jnp.sum(jnp.where(chosen, context_len[None, :], 0), axis=1) - DRAFT
    heads = queries.reshape(requests_dev, DRAFT, HEADS, LAT).transpose(0, 2, 1, 3)
    heads = heads.reshape(requests_dev, HEADS * DRAFT, LAT)
    query = jnp.pad(heads, ((0, 0), (0, 0), (0, SHIFT)))
    counts = jnp.minimum((limits + DRAFT - 1) // (2 * pairs) + 1, pages_each)
    plan = jnp.concatenate([counts, limits, place])
    latent_out = attend(plan, query, arrived.reshape(listed, pairs, 2 * LAT), pages_each)
    latent_out, last = lax.optimization_barrier((latent_out, last))
    moe_out = (residual.astype(jnp.float32) + mixed + last.astype(jnp.float32)).astype(jnp.bfloat16)
    return (latent_out, moe_out)


def solution(mesh):
    placed = (
        P(("rep", "ep", "sub"), None),
        P(("rep", "ep", "sub"), None),
        P("rep", None),
        P("rep"),
        P("rep"),
        P(("rep", "ep", "sub"), None),
        P(("rep", "ep", "sub"), None),
        P(("rep", "ep", "sub"), None),
        P("ep", None, "sub"),
        P("ep", None, "sub"),
        P("ep", "sub", None),
    )
    return jax.shard_map(
        local,
        mesh=mesh,
        in_specs=placed,
        out_specs=(P(("rep", "ep", "sub"), None), P(("rep", "ep", "sub"), None)),
        check_vma=False,
    )
```

```python
import functools
import math

import jax
import jax.numpy as jnp
from jax import lax
from jax.experimental import pallas as pl
from jax.experimental.pallas import tpu as pltpu
from jax.sharding import PartitionSpec as P

HEADS = 64
LAT = 576
KV = 512
DRAFT = 4
HALF = 640
SHIFT = HALF - LAT

exponent_scale = 192.0 ** (-0.5) * math.log2(math.e)
masked_score = -1e30
JOIN_FLOPS = 300_000_000_000
STAGE_FLOPS = 20_000_000_000


def ones_where(condition):
    return jnp.where(condition, 1.0, 0.0).astype(jnp.bfloat16)


def count(left, right):
    return jnp.dot(left, right, preferred_element_type=jnp.float32)


def stage_body(
    peers, device_ref, table_ref, serving_ref, pool_ref, out_ref, pool, pages, order, index, *sems
):
    pool_sem, order_sem, page_sems = sems
    fetch = pltpu.make_async_copy(pool_ref, pool, pool_sem)
    fetch.start()
    each, slots = table_ref.shape
    span = slots // peers
    fetched = out_ref.shape[0] // peers
    held = jnp.full((each, slots), pool.shape[0], jnp.int32)
    table = table_ref[...]
    named = ones_where(lax.broadcasted_iota(jnp.int32, (slots, slots), 0) == serving_ref[...])
    owner = count(lax.div(table, held).astype(jnp.float32).astype(jnp.bfloat16), named)
    place = count(lax.rem(table, held).astype(jnp.float32).astype(jnp.bfloat16), named)
    mine = owner == device_ref[0].astype(jnp.float32)
    flags = ones_where(mine)
    above = lax.broadcasted_iota(jnp.int32, (each, each), 1) < lax.broadcasted_iota(
        jnp.int32, (each, each), 0
    )
    first = lax.broadcasted_iota(jnp.int32, (slots, slots), 0)
    second = lax.broadcasted_iota(jnp.int32, (slots, slots), 1)
    spans = jnp.full((slots, slots), span, jnp.int32)
    before = (lax.div(first, spans) == lax.div(second, spans)) & (first < second)
    whole = jnp.ones((each, each), jnp.bfloat16)
    rank = count(ones_where(above), flags) + count(
        count(whole, flags).astype(jnp.bfloat16), ones_where(before)
    )
    serves = ones_where(
        lax.div(
            lax.broadcasted_iota(jnp.int32, (slots, peers), 0),
            jnp.full((slots, peers), span, jnp.int32),
        )
        == lax.broadcasted_iota(jnp.int32, (slots, peers), 1)
    )
    for k in range(fetched):
        chosen = jnp.where(mine & (rank == k), place, 0.0).astype(jnp.bfloat16)
        column = count(count(whole, chosen).astype(jnp.bfloat16), serves)
        order[k : k + 1, :peers] = column[:1].astype(jnp.int32)
    listing = pltpu.make_async_copy(order, index, order_sem)
    listing.start()
    fetch.wait()
    pages[...] = pool[...].reshape(pages.shape)
    listing.wait()

    def copy(p, k):
        slot = p * fetched + k
        return pltpu.make_async_copy(pages.at[index[k, p]], out_ref.at[slot], page_sems.at[slot])

    def begin(p, carry):
        for k in range(fetched):
            copy(p, k).start()
        return carry

    def finish(p, carry):
        for k in range(fetched):
            copy(p, k).wait()
        return carry

    lax.fori_loop(0, peers, begin, 0)
    lax.fori_loop(0, peers, finish, 0)


def stage_pages(device, table, serving, pool, peers, slots):
    pairs = pool.shape[1] // (2 * LAT)
    fetched = slots // peers
    listing = (fetched + -fetched % 8, peers + -peers % 128)
    return pl.pallas_call(
        functools.partial(stage_body, peers),
        out_shape=jax.ShapeDtypeStruct((slots, pairs, 2 * LAT), pool.dtype),
        in_specs=[
            pl.BlockSpec(memory_space=pltpu.SMEM),
            pl.BlockSpec(memory_space=pltpu.VMEM),
            pl.BlockSpec(memory_space=pltpu.VMEM),
            pl.BlockSpec(memory_space=pltpu.HBM),
        ],
        out_specs=pl.BlockSpec(memory_space=pltpu.HBM),
        scratch_shapes=[
            pltpu.VMEM(pool.shape, pool.dtype),
            pltpu.VMEM((pool.shape[0], pairs, 2 * LAT), pool.dtype),
            pltpu.VMEM(listing, jnp.int32),
            pltpu.SMEM(listing, jnp.int32),
            pltpu.SemaphoreType.DMA,
            pltpu.SemaphoreType.DMA,
            pltpu.SemaphoreType.DMA((slots,)),
        ],
        compiler_params=pltpu.CompilerParams(vmem_limit_bytes=56 << 20),
        cost_estimate=pl.CostEstimate(flops=STAGE_FLOPS, bytes_accessed=0, transcendentals=0),
        name="stage_pages",
    )(device, table, serving, pool)


def pack_body(experts, routes_ref, scores_ref, rows_ref, out_ref):
    top, rows = routes_ref.shape
    width = rows_ref.shape[1]
    scores = scores_ref[...]
    scaled = scores / jnp.sum(scores, axis=0, keepdims=True) * 2.5
    labels = lax.broadcasted_iota(jnp.int32, (experts, rows), 0)
    weights = jnp.zeros((experts, rows), jnp.float32)
    for k in range(top):
        weights += jnp.where(labels == routes_ref[k : k + 1, :], scaled[k : k + 1, :], 0.0)
    out_ref[:, :width] = rows_ref[...]
    side = jnp.zeros((rows, out_ref.shape[1] - width), jnp.float32)
    line = lax.broadcasted_iota(jnp.int32, (experts, side.shape[1]), 1)
    entry = lax.broadcasted_iota(jnp.int32, (experts, side.shape[1]), 0)
    for part in range(3):
        piece = weights.astype(jnp.bfloat16)
        weights = weights - piece.astype(jnp.float32)
        side += lax.dot_general(
            piece,
            ones_where(line == entry + part * experts),
            (((0,), (0,)), ((), ())),
            preferred_element_type=jnp.float32,
        )
    out_ref[:, width:] = side.astype(out_ref.dtype)


def pack_rows(routes, scores, rows, experts):
    side = 3 * experts
    width = rows.shape[1] + side + -side % 128
    return pl.pallas_call(
        functools.partial(pack_body, experts),
        out_shape=jax.ShapeDtypeStruct((rows.shape[0], width), rows.dtype),
        name="pack_rows",
    )(routes, scores, rows)


def join_body(*refs):
    blocks, out_ref = refs[:-1], refs[-1]
    start = 0
    for block_ref in blocks:
        out_ref[start : start + block_ref.shape[0], :] = block_ref[...]
        start += block_ref.shape[0]


def join_rows(blocks):
    rows = sum(block.shape[0] for block in blocks)
    return pl.pallas_call(
        join_body,
        out_shape=jax.ShapeDtypeStruct((rows, blocks[0].shape[1]), blocks[0].dtype),
        cost_estimate=pl.CostEstimate(flops=JOIN_FLOPS, bytes_accessed=0, transcendentals=0),
        name="join_rows",
    )(*blocks)


def exchange(block, group, bit):
    peers = lax.axis_size(group)
    return lax.ppermute(block, group, [(d, d ^ bit) for d in range(peers)])


def expert_body(experts, label_ref, kept_ref, other_ref, *refs):
    gate_hbm, up_hbm, down_hbm, kept_out, other_out, gate_ref, up_ref, down_ref, sems = refs
    copies = [
        pltpu.make_async_copy(gate_hbm, gate_ref, sems.at[0]),
        pltpu.make_async_copy(up_hbm, up_ref, sems.at[1]),
        pltpu.make_async_copy(down_hbm, down_ref, sems.at[2]),
    ]
    for weight_copy in copies:
        weight_copy.start()
    width = gate_ref.shape[0]
    parts = []
    copies[0].wait()
    for rows_ref in (other_ref, kept_ref):
        parts.append(jnp.dot(rows_ref[:, :width], gate_ref[...], preferred_element_type=jnp.float32))
    copies[1].wait()
    hiddens = []
    for rows_ref, gate in zip((other_ref, kept_ref), parts):
        upward = jnp.dot(rows_ref[:, :width], up_ref[...], preferred_element_type=jnp.float32)
        hiddens.append((gate / (1.0 + jnp.exp(-gate)) * upward).astype(jnp.bfloat16))
    copies[2].wait()
    for rows_ref, hidden, out_ref in zip((other_ref, kept_ref), hiddens, (other_out, kept_out)):
        side = rows_ref[:, width:].astype(jnp.float32)
        line = lax.broadcasted_iota(jnp.int32, side.shape, 1)
        mine = (line == label_ref[0]) | (line == label_ref[0] + experts)
        mine = mine | (line == label_ref[0] + 2 * experts)
        weight = jnp.sum(jnp.where(mine, side, 0.0), axis=1, keepdims=True)
        total = jnp.dot(hidden, down_ref[...], preferred_element_type=jnp.float32) * weight
        out_ref[...] = total.astype(out_ref.dtype)


def expert_rows(label, kept, other, gate, up, down, experts):
    return pl.pallas_call(
        functools.partial(expert_body, experts),
        out_shape=(
            jax.ShapeDtypeStruct((kept.shape[0], gate.shape[0]), jnp.float32),
            jax.ShapeDtypeStruct((other.shape[0], gate.shape[0]), jnp.bfloat16),
        ),
        in_specs=[pl.BlockSpec(memory_space=pltpu.SMEM)]
        + [pl.BlockSpec(memory_space=pltpu.VMEM)] * 2
        + [pl.BlockSpec(memory_space=pltpu.HBM)] * 3,
        scratch_shapes=[
            pltpu.VMEM(gate.shape, gate.dtype),
            pltpu.VMEM(up.shape, up.dtype),
            pltpu.VMEM(down.shape, down.dtype),
            pltpu.SemaphoreType.DMA((3,)),
        ],
        compiler_params=pltpu.CompilerParams(vmem_limit_bytes=56 << 20),
        cost_estimate=pl.CostEstimate(flops=0, bytes_accessed=0, transcendentals=0),
        name="expert_rows",
    )(label, kept, other, gate, up, down)


def attend_body(plan_ref, query_ref, pages_ref, out_ref, context, held, sems):
    requests, each, pairs, width = context.shape
    rows = query_ref.shape[1]
    contract = (((1,), (1,)), ((), ()))

    def copy(r, i):
        return pltpu.make_async_copy(
            pages_ref.at[plan_ref[2 * requests + r * each + i]], context.at[r, i], sems.at[r * each + i]
        )

    blank = jnp.zeros((pairs, width), context.dtype)
    for r in range(requests):

        def begin(i, carry, r=r):
            copy(r, i).start()
            return carry

        lax.fori_loop(0, plan_ref[r], begin, 0)
    for r in range(requests):

        def clear(i, carry, r=r):
            context[r, i] = blank
            return carry

        lax.fori_loop(plan_ref[r], each, clear, 0)

    columns = each * pairs
    draft = lax.broadcasted_iota(jnp.int32, (rows, columns), 0) % DRAFT
    early = 2 * lax.broadcasted_iota(jnp.int32, (rows, columns), 1) - draft

    def score(r):
        def finish(i, carry):
            copy(r, i).wait()
            return carry

        lax.fori_loop(0, plan_ref[r], finish, 0)
        block = context[r].reshape(columns, width)
        low = query_ref[r]
        high = pltpu.roll(low.astype(jnp.float32), SHIFT, 1).astype(low.dtype)
        even = lax.dot_general(
            low, block[:, :HALF], contract, preferred_element_type=jnp.float32
        )
        odd = lax.dot_general(
            high, block[:, width - HALF :], contract, preferred_element_type=jnp.float32
        )
        return even, odd

    scored = score(0)
    for r in range(requests):
        even, odd = scored
        if r + 1 < requests:
            scored = score(r + 1)
        limit = plan_ref[requests + r]
        even = jnp.where(early <= limit, even, masked_score)
        odd = jnp.where(early < limit, odd, masked_score)
        highest = jnp.max(jnp.maximum(even, odd), axis=-1, keepdims=True)
        even = jnp.exp2((even - highest) * exponent_scale)
        odd = jnp.exp2((odd - highest) * exponent_scale)
        total = jnp.sum(even + odd, axis=-1, keepdims=True)
        block = context[r].reshape(columns, width)
        latent = jnp.dot(
            even.astype(jnp.bfloat16), block[:, :KV], preferred_element_type=jnp.float32
        )
        other = jnp.dot(
            odd.astype(jnp.bfloat16), block[:, width - HALF :], preferred_element_type=jnp.float32
        )
        latent = (latent + other[:, SHIFT : SHIFT + KV]) * (1.0 / total)
        for h in range(rows // DRAFT):
            held[r * DRAFT : (r + 1) * DRAFT, h * KV : (h + 1) * KV] = latent[
                h * DRAFT : (h + 1) * DRAFT, :
            ]
    out_ref[...] = held[...].astype(out_ref.dtype)


def attend(plan, query, pages, each):
    requests, rows, _ = query.shape
    _, pairs, width = pages.shape
    out = (requests * DRAFT, (rows // DRAFT) * KV)
    return pl.pallas_call(
        attend_body,
        out_shape=jax.ShapeDtypeStruct(out, jnp.bfloat16),
        in_specs=[
            pl.BlockSpec(memory_space=pltpu.SMEM),
            pl.BlockSpec(memory_space=pltpu.VMEM),
            pl.BlockSpec(memory_space=pltpu.HBM),
        ],
        out_specs=pl.BlockSpec(memory_space=pltpu.VMEM),
        scratch_shapes=[
            pltpu.VMEM((requests, each, pairs, width), pages.dtype),
            pltpu.VMEM(out, jnp.float32),
            pltpu.SemaphoreType.DMA((requests * each,)),
        ],
        compiler_params=pltpu.CompilerParams(vmem_limit_bytes=50 << 20),
        name="attend_pages",
    )(plan, query, pages)


def local(
    queries,
    page_pool,
    page_table,
    serving,
    context_len,
    residual,
    routes,
    route_scores,
    w_gate,
    w_up,
    w_down,
):
    group = ("ep", "sub")
    peers = lax.axis_size(group)
    device = lax.axis_index(group)
    rows_dev, width = residual.shape
    requests_dev = rows_dev // DRAFT
    pages_each = page_table.shape[1]
    pool_pages = page_pool.shape[0]
    listed = requests_dev * pages_each
    fetched = listed // peers
    n_requests = serving.shape[0]

    n_ep = lax.axis_size("ep")
    experts = n_ep // 2
    packed = pack_rows(routes.T, route_scores.T, residual, experts)
    far, near = peers // 2, peers // 4
    across = [exchange(packed, group, bit) for bit in (far, near, far | near)]

    outgoing = stage_pages(
        device.reshape(1), page_table.T, serving.reshape(1, -1), page_pool, peers, listed
    )
    pairs = outgoing.shape[1]
    arrived = lax.all_to_all(
        outgoing.reshape(peers, fetched, pairs, 2 * LAT), group, split_axis=0, concat_axis=0, tiled=True
    )

    kept = join_rows([packed, *across])
    bit = near // 2
    while bit > 1:
        kept = jnp.concatenate([kept, exchange(kept, group, bit)], axis=0)
        bit //= 2
    kept, queries = lax.optimization_barrier((kept, queries))
    other = exchange(kept, group, 1)
    heads = queries.reshape(requests_dev, DRAFT, HEADS, LAT).transpose(0, 2, 1, 3)
    heads = heads.reshape(requests_dev, HEADS * DRAFT, LAT)
    query = jnp.pad(heads, ((0, 0), (0, 0), (0, SHIFT)))
    label = (lax.axis_index("ep") // 2).reshape(1)
    mixed, leaving = expert_rows(label, kept, other, w_gate[0], w_up[0], w_down[0], experts)
    bit = 1
    while True:
        last = exchange(leaving, group, bit)
        bit *= 2
        if bit == peers:
            break
        mixed = mixed + last.astype(jnp.float32)
        if bit == 2:
            mixed, query = lax.optimization_barrier((mixed, query))
        half = mixed.shape[0] // 2
        leaving = mixed[half:].astype(jnp.bfloat16)
        mixed = mixed[:half]

    served = lax.dynamic_slice_in_dim(serving, device * requests_dev, requests_dev)
    slots = jnp.arange(n_requests, dtype=jnp.int32)
    chosen = served[:, None] == slots[None, :]
    own_list = jnp.sum(jnp.where(chosen[:, :, None], page_table[None], 0), axis=1)
    own_list = own_list.reshape(-1) // pool_pages
    position = jnp.arange(listed, dtype=jnp.int32)
    same = (own_list[:, None] == own_list[None, :]) & (position[None, :] < position[:, None])
    place = own_list * fetched + jnp.sum(same.astype(jnp.int32), axis=1)
    limits = jnp.sum(jnp.where(chosen, context_len[None, :], 0), axis=1) - DRAFT
    counts = jnp.minimum((limits + DRAFT - 1) // (2 * pairs) + 1, pages_each)
    plan = jnp.concatenate([counts, limits, place])
    latent_out = attend(plan, query, arrived.reshape(listed, pairs, 2 * LAT), pages_each)
    latent_out, last = lax.optimization_barrier((latent_out, last))
    moe_out = (residual.astype(jnp.float32) + mixed + last.astype(jnp.float32)).astype(jnp.bfloat16)
    return (latent_out, moe_out)


def solution(mesh):
    placed = (
        P(("rep", "ep", "sub"), None),
        P(("rep", "ep", "sub"), None),
        P("rep", None),
        P("rep"),
        P("rep"),
        P(("rep", "ep", "sub"), None),
        P(("rep", "ep", "sub"), None),
        P(("rep", "ep", "sub"), None),
        P("ep", None, "sub"),
        P("ep", None, "sub"),
        P("ep", "sub", None),
    )
    return jax.shard_map(
        local,
        mesh=mesh,
        in_specs=placed,
        out_specs=(P(("rep", "ep", "sub"), None), P(("rep", "ep", "sub"), None)),
        check_vma=False,
    )
```

```python
import functools
import math

import jax
import jax.numpy as jnp
from jax import lax
from jax.experimental import pallas as pl
from jax.experimental.pallas import tpu as pltpu
from jax.sharding import PartitionSpec as P

HEADS = 64
LAT = 576
KV = 512
DRAFT = 4
HALF = 640
SHIFT = HALF - LAT

exponent_scale = 192.0 ** (-0.5) * math.log2(math.e)
masked_score = -1e30
JOIN_FLOPS = 300_000_000_000
STAGE_FLOPS = 20_000_000_000


def ones_where(condition):
    return jnp.where(condition, 1.0, 0.0).astype(jnp.bfloat16)


def count(left, right):
    return jnp.dot(left, right, preferred_element_type=jnp.float32)


def stage_body(
    peers, group, table_ref, serving_ref, pool_ref, out_ref, pool, pages, order, index, *sems
):
    table, serving, pool_sem, order_sem, table_sems, page_sems = sems
    fetch = pltpu.make_async_copy(pool_ref, pool, pool_sem)
    fetch_table = pltpu.make_async_copy(table_ref, table, table_sems.at[0])
    fetch_serving = pltpu.make_async_copy(serving_ref, serving, table_sems.at[1])
    fetch_table.start()
    fetch_serving.start()
    fetch.start()
    each, slots = table.shape
    span = slots // peers
    fetched = out_ref.shape[0] // peers
    fetch_table.wait()
    fetch_serving.wait()
    held = jnp.full((each, slots), pool.shape[0], jnp.int32)
    listed = table[...]
    named = ones_where(lax.broadcasted_iota(jnp.int32, (slots, slots), 0) == serving[...])
    owner = count(lax.div(listed, held).astype(jnp.float32).astype(jnp.bfloat16), named)
    place = count(lax.rem(listed, held).astype(jnp.float32).astype(jnp.bfloat16), named)
    device = lax.axis_index(group[0]) * lax.axis_size(group[1]) + lax.axis_index(group[1])
    mine = owner == device.astype(jnp.float32)
    flags = ones_where(mine)
    above = lax.broadcasted_iota(jnp.int32, (each, each), 1) < lax.broadcasted_iota(
        jnp.int32, (each, each), 0
    )
    first = lax.broadcasted_iota(jnp.int32, (slots, slots), 0)
    second = lax.broadcasted_iota(jnp.int32, (slots, slots), 1)
    spans = jnp.full((slots, slots), span, jnp.int32)
    before = (lax.div(first, spans) == lax.div(second, spans)) & (first < second)
    whole = jnp.ones((each, each), jnp.bfloat16)
    rank = count(ones_where(above), flags) + count(
        count(whole, flags).astype(jnp.bfloat16), ones_where(before)
    )
    serves = ones_where(
        lax.div(
            lax.broadcasted_iota(jnp.int32, (slots, peers), 0),
            jnp.full((slots, peers), span, jnp.int32),
        )
        == lax.broadcasted_iota(jnp.int32, (slots, peers), 1)
    )
    for k in range(fetched):
        chosen = jnp.where(mine & (rank == k), place, 0.0).astype(jnp.bfloat16)
        column = count(count(whole, chosen).astype(jnp.bfloat16), serves)
        order[k : k + 1, :peers] = column[:1].astype(jnp.int32)
    listing = pltpu.make_async_copy(order, index, order_sem)
    listing.start()
    fetch.wait()
    pages[...] = pool[...].reshape(pages.shape)
    listing.wait()

    def copy(p, k):
        slot = p * fetched + k
        return pltpu.make_async_copy(pages.at[index[k, p]], out_ref.at[slot], page_sems.at[slot])

    def begin(p, carry):
        for k in range(fetched):
            copy(p, k).start()
        return carry

    def finish(p, carry):
        for k in range(fetched):
            copy(p, k).wait()
        return carry

    lax.fori_loop(0, peers, begin, 0)
    lax.fori_loop(0, peers, finish, 0)


def stage_pages(group, table, serving, pool, peers, slots):
    pairs = pool.shape[1] // (2 * LAT)
    fetched = slots // peers
    listing = (fetched + -fetched % 8, peers + -peers % 128)
    return pl.pallas_call(
        functools.partial(stage_body, peers, group),
        out_shape=jax.ShapeDtypeStruct((slots, pairs, 2 * LAT), pool.dtype),
        in_specs=[pl.BlockSpec(memory_space=pltpu.HBM)] * 3,
        out_specs=pl.BlockSpec(memory_space=pltpu.HBM),
        scratch_shapes=[
            pltpu.VMEM(pool.shape, pool.dtype),
            pltpu.VMEM((pool.shape[0], pairs, 2 * LAT), pool.dtype),
            pltpu.VMEM(listing, jnp.int32),
            pltpu.SMEM(listing, jnp.int32),
            pltpu.VMEM(table.shape, table.dtype),
            pltpu.VMEM(serving.shape, serving.dtype),
            pltpu.SemaphoreType.DMA,
            pltpu.SemaphoreType.DMA,
            pltpu.SemaphoreType.DMA((2,)),
            pltpu.SemaphoreType.DMA((slots,)),
        ],
        compiler_params=pltpu.CompilerParams(vmem_limit_bytes=56 << 20),
        cost_estimate=pl.CostEstimate(flops=STAGE_FLOPS, bytes_accessed=0, transcendentals=0),
        name="stage_pages",
    )(table, serving, pool)


def pack_body(experts, routes_ref, scores_ref, rows_ref, out_ref):
    top, rows = routes_ref.shape
    width = rows_ref.shape[1]
    scores = scores_ref[...]
    scaled = scores / jnp.sum(scores, axis=0, keepdims=True) * 2.5
    labels = lax.broadcasted_iota(jnp.int32, (experts, rows), 0)
    weights = jnp.zeros((experts, rows), jnp.float32)
    for k in range(top):
        weights += jnp.where(labels == routes_ref[k : k + 1, :], scaled[k : k + 1, :], 0.0)
    out_ref[:, :width] = rows_ref[...]
    side = jnp.zeros((rows, out_ref.shape[1] - width), jnp.float32)
    line = lax.broadcasted_iota(jnp.int32, (experts, side.shape[1]), 1)
    entry = lax.broadcasted_iota(jnp.int32, (experts, side.shape[1]), 0)
    for part in range(3):
        piece = weights.astype(jnp.bfloat16)
        weights = weights - piece.astype(jnp.float32)
        side += lax.dot_general(
            piece,
            ones_where(line == entry + part * experts),
            (((0,), (0,)), ((), ())),
            preferred_element_type=jnp.float32,
        )
    out_ref[:, width:] = side.astype(out_ref.dtype)


def pack_rows(routes, scores, rows, experts):
    side = 3 * experts
    width = rows.shape[1] + side + -side % 128
    return pl.pallas_call(
        functools.partial(pack_body, experts),
        out_shape=jax.ShapeDtypeStruct((rows.shape[0], width), rows.dtype),
        name="pack_rows",
    )(routes, scores, rows)


def join_body(*refs):
    blocks, out_ref = refs[:-1], refs[-1]
    start = 0
    for block_ref in blocks:
        out_ref[start : start + block_ref.shape[0], :] = block_ref[...]
        start += block_ref.shape[0]


def join_rows(blocks):
    rows = sum(block.shape[0] for block in blocks)
    return pl.pallas_call(
        join_body,
        out_shape=jax.ShapeDtypeStruct((rows, blocks[0].shape[1]), blocks[0].dtype),
        cost_estimate=pl.CostEstimate(flops=JOIN_FLOPS, bytes_accessed=0, transcendentals=0),
        name="join_rows",
    )(*blocks)


def exchange(block, group, bit):
    peers = lax.axis_size(group)
    return lax.ppermute(block, group, [(d, d ^ bit) for d in range(peers)])


def expert_body(experts, label_ref, kept_ref, other_ref, *refs):
    gate_hbm, up_hbm, down_hbm, kept_out, other_out, gate_ref, up_ref, down_ref, sems = refs
    copies = [
        pltpu.make_async_copy(gate_hbm, gate_ref, sems.at[0]),
        pltpu.make_async_copy(up_hbm, up_ref, sems.at[1]),
        pltpu.make_async_copy(down_hbm, down_ref, sems.at[2]),
    ]
    for weight_copy in copies:
        weight_copy.start()
    width = gate_ref.shape[0]
    parts = []
    copies[0].wait()
    for rows_ref in (other_ref, kept_ref):
        parts.append(jnp.dot(rows_ref[:, :width], gate_ref[...], preferred_element_type=jnp.float32))
    copies[1].wait()
    hiddens = []
    for rows_ref, gate in zip((other_ref, kept_ref), parts):
        upward = jnp.dot(rows_ref[:, :width], up_ref[...], preferred_element_type=jnp.float32)
        hiddens.append((gate / (1.0 + jnp.exp(-gate)) * upward).astype(jnp.bfloat16))
    copies[2].wait()
    for rows_ref, hidden, out_ref in zip((other_ref, kept_ref), hiddens, (other_out, kept_out)):
        side = rows_ref[:, width:].astype(jnp.float32)
        line = lax.broadcasted_iota(jnp.int32, side.shape, 1)
        mine = (line == label_ref[0]) | (line == label_ref[0] + experts)
        mine = mine | (line == label_ref[0] + 2 * experts)
        weight = jnp.sum(jnp.where(mine, side, 0.0), axis=1, keepdims=True)
        total = jnp.dot(hidden, down_ref[...], preferred_element_type=jnp.float32) * weight
        out_ref[...] = total.astype(out_ref.dtype)


def expert_rows(label, kept, other, gate, up, down, experts):
    return pl.pallas_call(
        functools.partial(expert_body, experts),
        out_shape=(
            jax.ShapeDtypeStruct((kept.shape[0], gate.shape[0]), jnp.float32),
            jax.ShapeDtypeStruct((other.shape[0], gate.shape[0]), jnp.bfloat16),
        ),
        in_specs=[pl.BlockSpec(memory_space=pltpu.SMEM)]
        + [pl.BlockSpec(memory_space=pltpu.VMEM)] * 2
        + [pl.BlockSpec(memory_space=pltpu.HBM)] * 3,
        scratch_shapes=[
            pltpu.VMEM(gate.shape, gate.dtype),
            pltpu.VMEM(up.shape, up.dtype),
            pltpu.VMEM(down.shape, down.dtype),
            pltpu.SemaphoreType.DMA((3,)),
        ],
        compiler_params=pltpu.CompilerParams(vmem_limit_bytes=56 << 20),
        cost_estimate=pl.CostEstimate(flops=0, bytes_accessed=0, transcendentals=0),
        name="expert_rows",
    )(label, kept, other, gate, up, down)


def attend_body(plan_ref, query_ref, pages_ref, out_ref, context, held, sems):
    requests, each, pairs, width = context.shape
    rows = query_ref.shape[1]
    contract = (((1,), (1,)), ((), ()))

    def copy(r, i):
        return pltpu.make_async_copy(
            pages_ref.at[plan_ref[2 * requests + r * each + i]], context.at[r, i], sems.at[r * each + i]
        )

    blank = jnp.zeros((pairs, width), context.dtype)
    for r in range(requests):

        def begin(i, carry, r=r):
            copy(r, i).start()
            return carry

        lax.fori_loop(0, plan_ref[r], begin, 0)
    for r in range(requests):

        def clear(i, carry, r=r):
            context[r, i] = blank
            return carry

        lax.fori_loop(plan_ref[r], each, clear, 0)

    columns = each * pairs
    draft = lax.broadcasted_iota(jnp.int32, (rows, columns), 0) % DRAFT
    early = 2 * lax.broadcasted_iota(jnp.int32, (rows, columns), 1) - draft

    def score(r):
        def finish(i, carry):
            copy(r, i).wait()
            return carry

        lax.fori_loop(0, plan_ref[r], finish, 0)
        block = context[r].reshape(columns, width)
        low = query_ref[r]
        high = pltpu.roll(low.astype(jnp.float32), SHIFT, 1).astype(low.dtype)
        even = lax.dot_general(
            low, block[:, :HALF], contract, preferred_element_type=jnp.float32
        )
        odd = lax.dot_general(
            high, block[:, width - HALF :], contract, preferred_element_type=jnp.float32
        )
        return even, odd

    scored = score(0)
    for r in range(requests):
        even, odd = scored
        if r + 1 < requests:
            scored = score(r + 1)
        limit = plan_ref[requests + r]
        even = jnp.where(early <= limit, even, masked_score)
        odd = jnp.where(early < limit, odd, masked_score)
        highest = jnp.max(jnp.maximum(even, odd), axis=-1, keepdims=True)
        even = jnp.exp2((even - highest) * exponent_scale)
        odd = jnp.exp2((odd - highest) * exponent_scale)
        total = jnp.sum(even + odd, axis=-1, keepdims=True)
        block = context[r].reshape(columns, width)
        latent = jnp.dot(
            even.astype(jnp.bfloat16), block[:, :KV], preferred_element_type=jnp.float32
        )
        other = jnp.dot(
            odd.astype(jnp.bfloat16), block[:, width - HALF :], preferred_element_type=jnp.float32
        )
        latent = (latent + other[:, SHIFT : SHIFT + KV]) * (1.0 / total)
        for h in range(rows // DRAFT):
            held[r * DRAFT : (r + 1) * DRAFT, h * KV : (h + 1) * KV] = latent[
                h * DRAFT : (h + 1) * DRAFT, :
            ]
    out_ref[...] = held[...].astype(out_ref.dtype)


def attend(plan, query, pages, each):
    requests, rows, _ = query.shape
    _, pairs, width = pages.shape
    out = (requests * DRAFT, (rows // DRAFT) * KV)
    return pl.pallas_call(
        attend_body,
        out_shape=jax.ShapeDtypeStruct(out, jnp.bfloat16),
        in_specs=[
            pl.BlockSpec(memory_space=pltpu.SMEM),
            pl.BlockSpec(memory_space=pltpu.VMEM),
            pl.BlockSpec(memory_space=pltpu.HBM),
        ],
        out_specs=pl.BlockSpec(memory_space=pltpu.VMEM),
        scratch_shapes=[
            pltpu.VMEM((requests, each, pairs, width), pages.dtype),
            pltpu.VMEM(out, jnp.float32),
            pltpu.SemaphoreType.DMA((requests * each,)),
        ],
        compiler_params=pltpu.CompilerParams(vmem_limit_bytes=50 << 20),
        name="attend_pages",
    )(plan, query, pages)


def local(
    queries,
    page_pool,
    page_table,
    serving,
    context_len,
    residual,
    routes,
    route_scores,
    w_gate,
    w_up,
    w_down,
):
    group = ("ep", "sub")
    peers = lax.axis_size(group)
    device = lax.axis_index(group)
    rows_dev, width = residual.shape
    requests_dev = rows_dev // DRAFT
    pages_each = page_table.shape[1]
    pool_pages = page_pool.shape[0]
    listed = requests_dev * pages_each
    fetched = listed // peers
    n_requests = serving.shape[0]

    n_ep = lax.axis_size("ep")
    experts = n_ep // 2
    packed = pack_rows(routes.T, route_scores.T, residual, experts)
    far, near = peers // 2, peers // 4
    across = {bit: exchange(packed, group, bit) for bit in (far,)}

    outgoing = stage_pages(
        group, page_table.T, serving.reshape(1, -1), page_pool, peers, listed
    )
    later, outgoing = lax.optimization_barrier((packed, outgoing))
    across |= {bit: exchange(later, group, bit) for bit in (near, far | near,)}
    pairs = outgoing.shape[1]
    arrived = lax.all_to_all(
        outgoing.reshape(peers, fetched, pairs, 2 * LAT), group, split_axis=0, concat_axis=0, tiled=True
    )

    kept = join_rows([packed, across[far], across[near], across[far | near]])
    bit = near // 2
    while bit > 1:
        kept = jnp.concatenate([kept, exchange(kept, group, bit)], axis=0)
        bit //= 2
    kept, queries = lax.optimization_barrier((kept, queries))
    other = exchange(kept, group, 1)
    heads = queries.reshape(requests_dev, DRAFT, HEADS, LAT).transpose(0, 2, 1, 3)
    heads = heads.reshape(requests_dev, HEADS * DRAFT, LAT)
    query = jnp.pad(heads, ((0, 0), (0, 0), (0, SHIFT)))
    label = (lax.axis_index("ep") // 2).reshape(1)
    mixed, leaving = expert_rows(label, kept, other, w_gate[0], w_up[0], w_down[0], experts)
    bit = 1
    while True:
        last = exchange(leaving, group, bit)
        bit *= 2
        if bit == peers:
            break
        mixed = mixed + last.astype(jnp.float32)
        if bit == 2:
            mixed, query = lax.optimization_barrier((mixed, query))
        half = mixed.shape[0] // 2
        leaving = mixed[half:].astype(jnp.bfloat16)
        mixed = mixed[:half]

    served = lax.dynamic_slice_in_dim(serving, device * requests_dev, requests_dev)
    slots = jnp.arange(n_requests, dtype=jnp.int32)
    chosen = served[:, None] == slots[None, :]
    own_list = jnp.sum(jnp.where(chosen[:, :, None], page_table[None], 0), axis=1)
    own_list = own_list.reshape(-1) // pool_pages
    position = jnp.arange(listed, dtype=jnp.int32)
    same = (own_list[:, None] == own_list[None, :]) & (position[None, :] < position[:, None])
    place = own_list * fetched + jnp.sum(same.astype(jnp.int32), axis=1)
    limits = jnp.sum(jnp.where(chosen, context_len[None, :], 0), axis=1) - DRAFT
    counts = jnp.minimum((limits + DRAFT - 1) // (2 * pairs) + 1, pages_each)
    plan = jnp.concatenate([counts, limits, place])
    latent_out = attend(plan, query, arrived.reshape(listed, pairs, 2 * LAT), pages_each)
    latent_out, last = lax.optimization_barrier((latent_out, last))
    moe_out = (residual.astype(jnp.float32) + mixed + last.astype(jnp.float32)).astype(jnp.bfloat16)
    return (latent_out, moe_out)


def solution(mesh):
    placed = (
        P(("rep", "ep", "sub"), None),
        P(("rep", "ep", "sub"), None),
        P("rep", None),
        P("rep"),
        P("rep"),
        P(("rep", "ep", "sub"), None),
        P(("rep", "ep", "sub"), None),
        P(("rep", "ep", "sub"), None),
        P("ep", None, "sub"),
        P("ep", None, "sub"),
        P("ep", "sub", None),
    )
    return jax.shard_map(
        local,
        mesh=mesh,
        in_specs=placed,
        out_specs=(P(("rep", "ep", "sub"), None), P(("rep", "ep", "sub"), None)),
        check_vma=False,
    )
```

```python
import functools
import math

import jax
import jax.numpy as jnp
from jax import lax
from jax.experimental import pallas as pl
from jax.experimental.pallas import tpu as pltpu
from jax.sharding import PartitionSpec as P

HEADS = 64
LAT = 576
KV = 512
DRAFT = 4
HALF = 640
SHIFT = HALF - LAT

exponent_scale = 192.0 ** (-0.5) * math.log2(math.e)
masked_score = -1e30
JOIN_FLOPS = 300_000_000_000
STAGE_FLOPS = 20_000_000_000


def ones_where(condition):
    return jnp.where(condition, 1.0, 0.0).astype(jnp.bfloat16)


def count(left, right):
    return jnp.dot(left, right, preferred_element_type=jnp.float32)


def weigh(routes, scores, experts, lanes):
    top, rows = routes.shape
    scaled = scores / jnp.sum(scores, axis=0, keepdims=True) * 2.5
    labels = lax.broadcasted_iota(jnp.int32, (experts, rows), 0)
    weights = jnp.zeros((experts, rows), jnp.float32)
    for k in range(top):
        weights += jnp.where(labels == routes[k : k + 1, :], scaled[k : k + 1, :], 0.0)
    side = jnp.zeros((rows, lanes), jnp.float32)
    line = lax.broadcasted_iota(jnp.int32, (experts, lanes), 1)
    entry = lax.broadcasted_iota(jnp.int32, (experts, lanes), 0)
    for part in range(3):
        piece = weights.astype(jnp.bfloat16)
        weights = weights - piece.astype(jnp.float32)
        side += lax.dot_general(
            piece,
            ones_where(line == entry + part * experts),
            (((0,), (0,)), ((), ())),
            preferred_element_type=jnp.float32,
        )
    return side.astype(jnp.bfloat16)


def stage_body(peers, group, experts, table_ref, serving_ref, pool_ref, *refs):
    rows_hbm, routes_hbm, scores_hbm, out_ref, packed_ref, *refs = refs
    pool, pages, order, index, table, serving, packed, routes, scores, *sems = refs
    pool_sem, order_sem, table_sems, row_sems, page_sems = sems
    width = rows_hbm.shape[1]
    fetch = pltpu.make_async_copy(pool_ref, pool, pool_sem)
    fetch_table = pltpu.make_async_copy(table_ref, table, table_sems.at[0])
    fetch_serving = pltpu.make_async_copy(serving_ref, serving, table_sems.at[1])
    fetch_rows = [
        pltpu.make_async_copy(routes_hbm, routes, row_sems.at[0]),
        pltpu.make_async_copy(scores_hbm, scores, row_sems.at[1]),
        pltpu.make_async_copy(rows_hbm, packed.at[:, :width], row_sems.at[2]),
    ]
    send_rows = pltpu.make_async_copy(packed, packed_ref, row_sems.at[3])
    fetch_table.start()
    fetch_serving.start()
    for fetch_row in fetch_rows:
        fetch_row.start()
    fetch.start()
    each, slots = table.shape
    span = slots // peers
    fetched = out_ref.shape[0] // peers
    fetch_table.wait()
    fetch_serving.wait()
    held = jnp.full((each, slots), pool.shape[0], jnp.int32)
    listed = table[...]
    named = ones_where(lax.broadcasted_iota(jnp.int32, (slots, slots), 0) == serving[...])
    owner = count(lax.div(listed, held).astype(jnp.float32).astype(jnp.bfloat16), named)
    place = count(lax.rem(listed, held).astype(jnp.float32).astype(jnp.bfloat16), named)
    device = lax.axis_index(group[0]) * lax.axis_size(group[1]) + lax.axis_index(group[1])
    mine = owner == device.astype(jnp.float32)
    flags = ones_where(mine)
    above = lax.broadcasted_iota(jnp.int32, (each, each), 1) < lax.broadcasted_iota(
        jnp.int32, (each, each), 0
    )
    first = lax.broadcasted_iota(jnp.int32, (slots, slots), 0)
    second = lax.broadcasted_iota(jnp.int32, (slots, slots), 1)
    spans = jnp.full((slots, slots), span, jnp.int32)
    before = (lax.div(first, spans) == lax.div(second, spans)) & (first < second)
    whole = jnp.ones((each, each), jnp.bfloat16)
    rank = count(ones_where(above), flags) + count(
        count(whole, flags).astype(jnp.bfloat16), ones_where(before)
    )
    serves = ones_where(
        lax.div(
            lax.broadcasted_iota(jnp.int32, (slots, peers), 0),
            jnp.full((slots, peers), span, jnp.int32),
        )
        == lax.broadcasted_iota(jnp.int32, (slots, peers), 1)
    )
    for k in range(fetched):
        chosen = jnp.where(mine & (rank == k), place, 0.0).astype(jnp.bfloat16)
        column = count(count(whole, chosen).astype(jnp.bfloat16), serves)
        order[k : k + 1, :peers] = column[:1].astype(jnp.int32)
    listing = pltpu.make_async_copy(order, index, order_sem)
    listing.start()
    for fetch_row in fetch_rows:
        fetch_row.wait()
    packed[:, width:] = weigh(routes[...], scores[...], experts, packed.shape[1] - width)
    send_rows.start()
    fetch.wait()
    pages[...] = pool[...].reshape(pages.shape)
    listing.wait()

    def copy(p, k):
        slot = p * fetched + k
        return pltpu.make_async_copy(pages.at[index[k, p]], out_ref.at[slot], page_sems.at[slot])

    def begin(p, carry):
        for k in range(fetched):
            copy(p, k).start()
        return carry

    def finish(p, carry):
        for k in range(fetched):
            copy(p, k).wait()
        return carry

    lax.fori_loop(0, peers, begin, 0)
    send_rows.wait()
    lax.fori_loop(0, peers, finish, 0)


def stage_pages(group, table, serving, pool, rows, routes, scores, peers, slots, experts):
    side = 3 * experts
    packed = (rows.shape[0], rows.shape[1] + side + -side % 128)
    pairs = pool.shape[1] // (2 * LAT)
    fetched = slots // peers
    listing = (fetched + -fetched % 8, peers + -peers % 128)
    return pl.pallas_call(
        functools.partial(stage_body, peers, group, experts),
        out_shape=(
            jax.ShapeDtypeStruct((slots, pairs, 2 * LAT), pool.dtype),
            jax.ShapeDtypeStruct(packed, rows.dtype),
        ),
        in_specs=[pl.BlockSpec(memory_space=pltpu.HBM)] * 6,
        out_specs=(pl.BlockSpec(memory_space=pltpu.HBM),) * 2,
        scratch_shapes=[
            pltpu.VMEM(pool.shape, pool.dtype),
            pltpu.VMEM((pool.shape[0], pairs, 2 * LAT), pool.dtype),
            pltpu.VMEM(listing, jnp.int32),
            pltpu.SMEM(listing, jnp.int32),
            pltpu.VMEM(table.shape, table.dtype),
            pltpu.VMEM(serving.shape, serving.dtype),
            pltpu.VMEM(packed, rows.dtype),
            pltpu.VMEM(routes.shape, routes.dtype),
            pltpu.VMEM(scores.shape, scores.dtype),
            pltpu.SemaphoreType.DMA,
            pltpu.SemaphoreType.DMA,
            pltpu.SemaphoreType.DMA((2,)),
            pltpu.SemaphoreType.DMA((4,)),
            pltpu.SemaphoreType.DMA((slots,)),
        ],
        compiler_params=pltpu.CompilerParams(vmem_limit_bytes=56 << 20),
        cost_estimate=pl.CostEstimate(flops=STAGE_FLOPS, bytes_accessed=0, transcendentals=0),
        name="stage_pages",
    )(table, serving, pool, rows, routes, scores)


def join_body(*refs):
    blocks, out_ref = refs[:-1], refs[-1]
    start = 0
    for block_ref in blocks:
        out_ref[start : start + block_ref.shape[0], :] = block_ref[...]
        start += block_ref.shape[0]


def join_rows(blocks):
    rows = sum(block.shape[0] for block in blocks)
    return pl.pallas_call(
        join_body,
        out_shape=jax.ShapeDtypeStruct((rows, blocks[0].shape[1]), blocks[0].dtype),
        cost_estimate=pl.CostEstimate(flops=JOIN_FLOPS, bytes_accessed=0, transcendentals=0),
        name="join_rows",
    )(*blocks)


def exchange(block, group, bit):
    peers = lax.axis_size(group)
    return lax.ppermute(block, group, [(d, d ^ bit) for d in range(peers)])


def expert_body(experts, label_ref, kept_ref, other_ref, *refs):
    gate_hbm, up_hbm, down_hbm, kept_out, other_out, gate_ref, up_ref, down_ref, sems = refs
    copies = [
        pltpu.make_async_copy(gate_hbm, gate_ref, sems.at[0]),
        pltpu.make_async_copy(up_hbm, up_ref, sems.at[1]),
        pltpu.make_async_copy(down_hbm, down_ref, sems.at[2]),
    ]
    for weight_copy in copies:
        weight_copy.start()
    width = gate_ref.shape[0]
    parts = []
    copies[0].wait()
    for rows_ref in (other_ref, kept_ref):
        parts.append(jnp.dot(rows_ref[:, :width], gate_ref[...], preferred_element_type=jnp.float32))
    copies[1].wait()
    hiddens = []
    for rows_ref, gate in zip((other_ref, kept_ref), parts):
        upward = jnp.dot(rows_ref[:, :width], up_ref[...], preferred_element_type=jnp.float32)
        hiddens.append((gate / (1.0 + jnp.exp(-gate)) * upward).astype(jnp.bfloat16))
    copies[2].wait()
    for rows_ref, hidden, out_ref in zip((other_ref, kept_ref), hiddens, (other_out, kept_out)):
        side = rows_ref[:, width:].astype(jnp.float32)
        line = lax.broadcasted_iota(jnp.int32, side.shape, 1)
        mine = (line == label_ref[0]) | (line == label_ref[0] + experts)
        mine = mine | (line == label_ref[0] + 2 * experts)
        weight = jnp.sum(jnp.where(mine, side, 0.0), axis=1, keepdims=True)
        total = jnp.dot(hidden, down_ref[...], preferred_element_type=jnp.float32) * weight
        out_ref[...] = total.astype(out_ref.dtype)


def expert_rows(label, kept, other, gate, up, down, experts):
    return pl.pallas_call(
        functools.partial(expert_body, experts),
        out_shape=(
            jax.ShapeDtypeStruct((kept.shape[0], gate.shape[0]), jnp.float32),
            jax.ShapeDtypeStruct((other.shape[0], gate.shape[0]), jnp.bfloat16),
        ),
        in_specs=[pl.BlockSpec(memory_space=pltpu.SMEM)]
        + [pl.BlockSpec(memory_space=pltpu.VMEM)] * 2
        + [pl.BlockSpec(memory_space=pltpu.HBM)] * 3,
        scratch_shapes=[
            pltpu.VMEM(gate.shape, gate.dtype),
            pltpu.VMEM(up.shape, up.dtype),
            pltpu.VMEM(down.shape, down.dtype),
            pltpu.SemaphoreType.DMA((3,)),
        ],
        compiler_params=pltpu.CompilerParams(vmem_limit_bytes=56 << 20),
        cost_estimate=pl.CostEstimate(flops=0, bytes_accessed=0, transcendentals=0),
        name="expert_rows",
    )(label, kept, other, gate, up, down)


def attend_body(plan_ref, query_ref, pages_ref, out_ref, context, held, sems):
    requests, each, pairs, width = context.shape
    rows = query_ref.shape[1]
    contract = (((1,), (1,)), ((), ()))

    def copy(r, i):
        return pltpu.make_async_copy(
            pages_ref.at[plan_ref[2 * requests + r * each + i]], context.at[r, i], sems.at[r * each + i]
        )

    blank = jnp.zeros((pairs, width), context.dtype)
    for r in range(requests):

        def begin(i, carry, r=r):
            copy(r, i).start()
            return carry

        lax.fori_loop(0, plan_ref[r], begin, 0)
    for r in range(requests):

        def clear(i, carry, r=r):
            context[r, i] = blank
            return carry

        lax.fori_loop(plan_ref[r], each, clear, 0)

    columns = each * pairs
    draft = lax.broadcasted_iota(jnp.int32, (rows, columns), 0) % DRAFT
    early = 2 * lax.broadcasted_iota(jnp.int32, (rows, columns), 1) - draft

    def score(r):
        def finish(i, carry):
            copy(r, i).wait()
            return carry

        lax.fori_loop(0, plan_ref[r], finish, 0)
        block = context[r].reshape(columns, width)
        low = query_ref[r]
        high = pltpu.roll(low.astype(jnp.float32), SHIFT, 1).astype(low.dtype)
        even = lax.dot_general(
            low, block[:, :HALF], contract, preferred_element_type=jnp.float32
        )
        odd = lax.dot_general(
            high, block[:, width - HALF :], contract, preferred_element_type=jnp.float32
        )
        return even, odd

    scored = score(0)
    for r in range(requests):
        even, odd = scored
        if r + 1 < requests:
            scored = score(r + 1)
        limit = plan_ref[requests + r]
        even = jnp.where(early <= limit, even, masked_score)
        odd = jnp.where(early < limit, odd, masked_score)
        highest = jnp.max(jnp.maximum(even, odd), axis=-1, keepdims=True)
        even = jnp.exp2((even - highest) * exponent_scale)
        odd = jnp.exp2((odd - highest) * exponent_scale)
        total = jnp.sum(even + odd, axis=-1, keepdims=True)
        block = context[r].reshape(columns, width)
        latent = jnp.dot(
            even.astype(jnp.bfloat16), block[:, :KV], preferred_element_type=jnp.float32
        )
        other = jnp.dot(
            odd.astype(jnp.bfloat16), block[:, width - HALF :], preferred_element_type=jnp.float32
        )
        latent = (latent + other[:, SHIFT : SHIFT + KV]) * (1.0 / total)
        for h in range(rows // DRAFT):
            held[r * DRAFT : (r + 1) * DRAFT, h * KV : (h + 1) * KV] = latent[
                h * DRAFT : (h + 1) * DRAFT, :
            ]
    out_ref[...] = held[...].astype(out_ref.dtype)


def attend(plan, query, pages, each):
    requests, rows, _ = query.shape
    _, pairs, width = pages.shape
    out = (requests * DRAFT, (rows // DRAFT) * KV)
    return pl.pallas_call(
        attend_body,
        out_shape=jax.ShapeDtypeStruct(out, jnp.bfloat16),
        in_specs=[
            pl.BlockSpec(memory_space=pltpu.SMEM),
            pl.BlockSpec(memory_space=pltpu.VMEM),
            pl.BlockSpec(memory_space=pltpu.HBM),
        ],
        out_specs=pl.BlockSpec(memory_space=pltpu.VMEM),
        scratch_shapes=[
            pltpu.VMEM((requests, each, pairs, width), pages.dtype),
            pltpu.VMEM(out, jnp.float32),
            pltpu.SemaphoreType.DMA((requests * each,)),
        ],
        compiler_params=pltpu.CompilerParams(vmem_limit_bytes=50 << 20),
        name="attend_pages",
    )(plan, query, pages)


def local(
    queries,
    page_pool,
    page_table,
    serving,
    context_len,
    residual,
    routes,
    route_scores,
    w_gate,
    w_up,
    w_down,
):
    group = ("ep", "sub")
    peers = lax.axis_size(group)
    device = lax.axis_index(group)
    rows_dev, width = residual.shape
    requests_dev = rows_dev // DRAFT
    pages_each = page_table.shape[1]
    pool_pages = page_pool.shape[0]
    listed = requests_dev * pages_each
    fetched = listed // peers
    n_requests = serving.shape[0]

    n_ep = lax.axis_size("ep")
    experts = n_ep // 2
    far, near = peers // 2, peers // 4

    outgoing, packed = stage_pages(
        group,
        page_table.T,
        serving.reshape(1, -1),
        page_pool,
        residual,
        routes.T,
        route_scores.T,
        peers,
        listed,
        experts,
    )
    across = [exchange(packed, group, bit) for bit in (far, far | near, near)]
    pairs = outgoing.shape[1]
    arrived = lax.all_to_all(
        outgoing.reshape(peers, fetched, pairs, 2 * LAT), group, split_axis=0, concat_axis=0, tiled=True
    )

    kept = join_rows([packed, across[0], across[2], across[1]])
    bit = near // 2
    while bit > 1:
        kept = jnp.concatenate([kept, exchange(kept, group, bit)], axis=0)
        bit //= 2
    kept, queries = lax.optimization_barrier((kept, queries))
    other = exchange(kept, group, 1)
    heads = queries.reshape(requests_dev, DRAFT, HEADS, LAT).transpose(0, 2, 1, 3)
    heads = heads.reshape(requests_dev, HEADS * DRAFT, LAT)
    query = jnp.pad(heads, ((0, 0), (0, 0), (0, SHIFT)))
    label = (lax.axis_index("ep") // 2).reshape(1)
    mixed, leaving = expert_rows(label, kept, other, w_gate[0], w_up[0], w_down[0], experts)
    bit = 1
    while True:
        last = exchange(leaving, group, bit)
        bit *= 2
        if bit == peers:
            break
        mixed = mixed + last.astype(jnp.float32)
        if bit == 2:
            mixed, query = lax.optimization_barrier((mixed, query))
        half = mixed.shape[0] // 2
        leaving = mixed[half:].astype(jnp.bfloat16)
        mixed = mixed[:half]

    served = lax.dynamic_slice_in_dim(serving, device * requests_dev, requests_dev)
    slots = jnp.arange(n_requests, dtype=jnp.int32)
    chosen = served[:, None] == slots[None, :]
    own_list = jnp.sum(jnp.where(chosen[:, :, None], page_table[None], 0), axis=1)
    own_list = own_list.reshape(-1) // pool_pages
    position = jnp.arange(listed, dtype=jnp.int32)
    same = (own_list[:, None] == own_list[None, :]) & (position[None, :] < position[:, None])
    place = own_list * fetched + jnp.sum(same.astype(jnp.int32), axis=1)
    limits = jnp.sum(jnp.where(chosen, context_len[None, :], 0), axis=1) - DRAFT
    counts = jnp.minimum((limits + DRAFT - 1) // (2 * pairs) + 1, pages_each)
    plan = jnp.concatenate([counts, limits, place])
    latent_out = attend(plan, query, arrived.reshape(listed, pairs, 2 * LAT), pages_each)
    latent_out, last = lax.optimization_barrier((latent_out, last))
    moe_out = (residual.astype(jnp.float32) + mixed + last.astype(jnp.float32)).astype(jnp.bfloat16)
    return (latent_out, moe_out)


def solution(mesh):
    placed = (
        P(("rep", "ep", "sub"), None),
        P(("rep", "ep", "sub"), None),
        P("rep", None),
        P("rep"),
        P("rep"),
        P(("rep", "ep", "sub"), None),
        P(("rep", "ep", "sub"), None),
        P(("rep", "ep", "sub"), None),
        P("ep", None, "sub"),
        P("ep", None, "sub"),
        P("ep", "sub", None),
    )
    return jax.shard_map(
        local,
        mesh=mesh,
        in_specs=placed,
        out_specs=(P(("rep", "ep", "sub"), None), P(("rep", "ep", "sub"), None)),
        check_vma=False,
    )
```

```python
import functools
import math

import jax
import jax.numpy as jnp
from jax import lax
from jax.experimental import pallas as pl
from jax.experimental.pallas import tpu as pltpu
from jax.sharding import PartitionSpec as P

HEADS = 64
LAT = 576
KV = 512
DRAFT = 4
HALF = 640
SHIFT = HALF - LAT

exponent_scale = 192.0 ** (-0.5) * math.log2(math.e)
masked_score = -1e30
JOIN_FLOPS = 300_000_000_000
STAGE_FLOPS = 20_000_000_000


def ones_where(condition):
    return jnp.where(condition, 1.0, 0.0).astype(jnp.bfloat16)


def count(left, right):
    return jnp.dot(left, right, preferred_element_type=jnp.float32)


def weigh(routes, scores, experts, lanes):
    top, rows = routes.shape
    scaled = scores / jnp.sum(scores, axis=0, keepdims=True) * 2.5
    labels = lax.broadcasted_iota(jnp.int32, (experts, rows), 0)
    weights = jnp.zeros((experts, rows), jnp.float32)
    for k in range(top):
        weights += jnp.where(labels == routes[k : k + 1, :], scaled[k : k + 1, :], 0.0)
    side = jnp.zeros((rows, lanes), jnp.float32)
    line = lax.broadcasted_iota(jnp.int32, (experts, lanes), 1)
    entry = lax.broadcasted_iota(jnp.int32, (experts, lanes), 0)
    for part in range(3):
        piece = weights.astype(jnp.bfloat16)
        weights = weights - piece.astype(jnp.float32)
        side += lax.dot_general(
            piece,
            ones_where(line == entry + part * experts),
            (((0,), (0,)), ((), ())),
            preferred_element_type=jnp.float32,
        )
    return side.astype(jnp.bfloat16)


def stage_body(peers, group, experts, table_ref, serving_ref, pool_ref, *refs):
    rows_hbm, routes_hbm, scores_hbm, out_ref, packed_ref, *refs = refs
    pool, pages, order, index, table, serving, packed, routes, scores, *sems = refs
    pool_sem, order_sem, table_sems, row_sems, page_sem = sems
    width = rows_hbm.shape[1]
    fetch = pltpu.make_async_copy(pool_ref, pool, pool_sem)
    fetch_table = pltpu.make_async_copy(table_ref, table, table_sems.at[0])
    fetch_serving = pltpu.make_async_copy(serving_ref, serving, table_sems.at[1])
    fetch_rows = [
        pltpu.make_async_copy(routes_hbm, routes, row_sems.at[0]),
        pltpu.make_async_copy(scores_hbm, scores, row_sems.at[1]),
        pltpu.make_async_copy(rows_hbm, packed.at[:, :width], row_sems.at[2]),
    ]
    send_rows = pltpu.make_async_copy(packed, packed_ref, row_sems.at[3])
    fetch_table.start()
    fetch_serving.start()
    for fetch_row in fetch_rows:
        fetch_row.start()
    fetch.start()
    each, slots = table.shape
    span = slots // peers
    fetched = out_ref.shape[0] // peers
    fetch_table.wait()
    fetch_serving.wait()
    held = jnp.full((each, slots), pool.shape[0], jnp.int32)
    listed = table[...]
    named = ones_where(lax.broadcasted_iota(jnp.int32, (slots, slots), 0) == serving[...])
    owner = count(lax.div(listed, held).astype(jnp.float32).astype(jnp.bfloat16), named)
    place = count(lax.rem(listed, held).astype(jnp.float32).astype(jnp.bfloat16), named)
    device = lax.axis_index(group[0]) * lax.axis_size(group[1]) + lax.axis_index(group[1])
    mine = owner == device.astype(jnp.float32)
    flags = ones_where(mine)
    above = lax.broadcasted_iota(jnp.int32, (each, each), 1) < lax.broadcasted_iota(
        jnp.int32, (each, each), 0
    )
    first = lax.broadcasted_iota(jnp.int32, (slots, slots), 0)
    second = lax.broadcasted_iota(jnp.int32, (slots, slots), 1)
    spans = jnp.full((slots, slots), span, jnp.int32)
    before = (lax.div(first, spans) == lax.div(second, spans)) & (first < second)
    whole = jnp.ones((each, each), jnp.bfloat16)
    rank = count(ones_where(above), flags) + count(
        count(whole, flags).astype(jnp.bfloat16), ones_where(before)
    )
    serves = ones_where(
        lax.div(
            lax.broadcasted_iota(jnp.int32, (slots, peers), 0),
            jnp.full((slots, peers), span, jnp.int32),
        )
        == lax.broadcasted_iota(jnp.int32, (slots, peers), 1)
    )
    for k in range(fetched):
        chosen = jnp.where(mine & (rank == k), place, 0.0).astype(jnp.bfloat16)
        column = count(count(whole, chosen).astype(jnp.bfloat16), serves)
        order[k : k + 1, :peers] = column[:1].astype(jnp.int32)
    listing = pltpu.make_async_copy(order, index, order_sem)
    listing.start()
    for fetch_row in fetch_rows:
        fetch_row.wait()
    packed[:, width:] = weigh(routes[...], scores[...], experts, packed.shape[1] - width)
    send_rows.start()
    fetch.wait()
    pages[...] = pool[...].reshape(pages.shape)
    listing.wait()

    def begin(p, carry):
        for k in range(fetched):
            pltpu.make_async_copy(
                pages.at[index[k, p]], out_ref.at[p * fetched + k], page_sem
            ).start()
        return carry

    lax.fori_loop(0, peers, begin, 0, unroll=4)
    send_rows.wait()
    pltpu.make_async_copy(out_ref, out_ref, page_sem).wait()


def stage_pages(group, table, serving, pool, rows, routes, scores, peers, slots, experts):
    side = 3 * experts
    packed = (rows.shape[0], rows.shape[1] + side + -side % 128)
    pairs = pool.shape[1] // (2 * LAT)
    fetched = slots // peers
    listing = (fetched + -fetched % 8, peers + -peers % 128)
    return pl.pallas_call(
        functools.partial(stage_body, peers, group, experts),
        out_shape=(
            jax.ShapeDtypeStruct((slots, pairs, 2 * LAT), pool.dtype),
            jax.ShapeDtypeStruct(packed, rows.dtype),
        ),
        in_specs=[pl.BlockSpec(memory_space=pltpu.HBM)] * 6,
        out_specs=(pl.BlockSpec(memory_space=pltpu.HBM),) * 2,
        scratch_shapes=[
            pltpu.VMEM(pool.shape, pool.dtype),
            pltpu.VMEM((pool.shape[0], pairs, 2 * LAT), pool.dtype),
            pltpu.VMEM(listing, jnp.int32),
            pltpu.SMEM(listing, jnp.int32),
            pltpu.VMEM(table.shape, table.dtype),
            pltpu.VMEM(serving.shape, serving.dtype),
            pltpu.VMEM(packed, rows.dtype),
            pltpu.VMEM(routes.shape, routes.dtype),
            pltpu.VMEM(scores.shape, scores.dtype),
            pltpu.SemaphoreType.DMA,
            pltpu.SemaphoreType.DMA,
            pltpu.SemaphoreType.DMA((2,)),
            pltpu.SemaphoreType.DMA((4,)),
            pltpu.SemaphoreType.DMA,
        ],
        compiler_params=pltpu.CompilerParams(vmem_limit_bytes=56 << 20),
        cost_estimate=pl.CostEstimate(flops=STAGE_FLOPS, bytes_accessed=0, transcendentals=0),
        name="stage_pages",
    )(table, serving, pool, rows, routes, scores)


def join_body(*refs):
    blocks, out_ref = refs[:-1], refs[-1]
    start = 0
    for block_ref in blocks:
        out_ref[start : start + block_ref.shape[0], :] = block_ref[...]
        start += block_ref.shape[0]


def join_rows(blocks):
    rows = sum(block.shape[0] for block in blocks)
    return pl.pallas_call(
        join_body,
        out_shape=jax.ShapeDtypeStruct((rows, blocks[0].shape[1]), blocks[0].dtype),
        cost_estimate=pl.CostEstimate(flops=JOIN_FLOPS, bytes_accessed=0, transcendentals=0),
        name="join_rows",
    )(*blocks)


def exchange(block, group, bit):
    peers = lax.axis_size(group)
    return lax.ppermute(block, group, [(d, d ^ bit) for d in range(peers)])


def expert_body(experts, label_ref, kept_ref, other_ref, *refs):
    gate_hbm, up_hbm, down_hbm, kept_out, other_out, gate_ref, up_ref, down_ref, sems = refs
    copies = [
        pltpu.make_async_copy(gate_hbm, gate_ref, sems.at[0]),
        pltpu.make_async_copy(up_hbm, up_ref, sems.at[1]),
        pltpu.make_async_copy(down_hbm, down_ref, sems.at[2]),
    ]
    for weight_copy in copies:
        weight_copy.start()
    width = gate_ref.shape[0]
    parts = []
    copies[0].wait()
    for rows_ref in (other_ref, kept_ref):
        parts.append(jnp.dot(rows_ref[:, :width], gate_ref[...], preferred_element_type=jnp.float32))
    copies[1].wait()
    hiddens = []
    for rows_ref, gate in zip((other_ref, kept_ref), parts):
        upward = jnp.dot(rows_ref[:, :width], up_ref[...], preferred_element_type=jnp.float32)
        hiddens.append((gate / (1.0 + jnp.exp(-gate)) * upward).astype(jnp.bfloat16))
    copies[2].wait()
    for rows_ref, hidden, out_ref in zip((other_ref, kept_ref), hiddens, (other_out, kept_out)):
        side = rows_ref[:, width:].astype(jnp.float32)
        line = lax.broadcasted_iota(jnp.int32, side.shape, 1)
        mine = (line == label_ref[0]) | (line == label_ref[0] + experts)
        mine = mine | (line == label_ref[0] + 2 * experts)
        weight = jnp.sum(jnp.where(mine, side, 0.0), axis=1, keepdims=True)
        total = jnp.dot(hidden, down_ref[...], preferred_element_type=jnp.float32) * weight
        out_ref[...] = total.astype(out_ref.dtype)


def expert_rows(label, kept, other, gate, up, down, experts):
    return pl.pallas_call(
        functools.partial(expert_body, experts),
        out_shape=(
            jax.ShapeDtypeStruct((kept.shape[0], gate.shape[0]), jnp.float32),
            jax.ShapeDtypeStruct((other.shape[0], gate.shape[0]), jnp.bfloat16),
        ),
        in_specs=[pl.BlockSpec(memory_space=pltpu.SMEM)]
        + [pl.BlockSpec(memory_space=pltpu.VMEM)] * 2
        + [pl.BlockSpec(memory_space=pltpu.HBM)] * 3,
        scratch_shapes=[
            pltpu.VMEM(gate.shape, gate.dtype),
            pltpu.VMEM(up.shape, up.dtype),
            pltpu.VMEM(down.shape, down.dtype),
            pltpu.SemaphoreType.DMA((3,)),
        ],
        compiler_params=pltpu.CompilerParams(vmem_limit_bytes=56 << 20),
        cost_estimate=pl.CostEstimate(flops=0, bytes_accessed=0, transcendentals=0),
        name="expert_rows",
    )(label, kept, other, gate, up, down)


def attend_body(plan_ref, query_ref, pages_ref, out_ref, context, held, sems):
    requests, each, pairs, width = context.shape
    rows = query_ref.shape[1]
    contract = (((1,), (1,)), ((), ()))

    for r in range(requests):

        def begin(i, carry, r=r):
            pltpu.make_async_copy(
                pages_ref.at[plan_ref[requests + r * each + i]], context.at[r, i], sems.at[r]
            ).start()
            return carry

        lax.fori_loop(0, each, begin, 0, unroll=4)

    columns = each * pairs
    draft = lax.broadcasted_iota(jnp.int32, (rows, columns), 0) % DRAFT
    early = 2 * lax.broadcasted_iota(jnp.int32, (rows, columns), 1) - draft

    def score(r):
        pltpu.make_async_copy(context.at[r], context.at[r], sems.at[r]).wait()
        block = context[r].reshape(columns, width)
        low = query_ref[r]
        high = pltpu.roll(low.astype(jnp.float32), SHIFT, 1).astype(low.dtype)
        even = lax.dot_general(
            low, block[:, :HALF], contract, preferred_element_type=jnp.float32
        )
        odd = lax.dot_general(
            high, block[:, width - HALF :], contract, preferred_element_type=jnp.float32
        )
        return even, odd

    scored = score(0)
    for r in range(requests):
        even, odd = scored
        if r + 1 < requests:
            scored = score(r + 1)
        limit = plan_ref[r]
        even = jnp.where(early <= limit, even, masked_score)
        odd = jnp.where(early < limit, odd, masked_score)
        highest = jnp.max(jnp.maximum(even, odd), axis=-1, keepdims=True)
        even = jnp.exp2((even - highest) * exponent_scale)
        odd = jnp.exp2((odd - highest) * exponent_scale)
        total = jnp.sum(even + odd, axis=-1, keepdims=True)
        block = context[r].reshape(columns, width)
        latent = jnp.dot(
            even.astype(jnp.bfloat16), block[:, :KV], preferred_element_type=jnp.float32
        )
        other = jnp.dot(
            odd.astype(jnp.bfloat16), block[:, width - HALF :], preferred_element_type=jnp.float32
        )
        latent = (latent + other[:, SHIFT : SHIFT + KV]) * (1.0 / total)
        for h in range(rows // DRAFT):
            held[r * DRAFT : (r + 1) * DRAFT, h * KV : (h + 1) * KV] = latent[
                h * DRAFT : (h + 1) * DRAFT, :
            ]
    out_ref[...] = held[...].astype(out_ref.dtype)


def attend(plan, query, pages, each):
    requests, rows, _ = query.shape
    _, pairs, width = pages.shape
    out = (requests * DRAFT, (rows // DRAFT) * KV)
    return pl.pallas_call(
        attend_body,
        out_shape=jax.ShapeDtypeStruct(out, jnp.bfloat16),
        in_specs=[
            pl.BlockSpec(memory_space=pltpu.SMEM),
            pl.BlockSpec(memory_space=pltpu.VMEM),
            pl.BlockSpec(memory_space=pltpu.HBM),
        ],
        out_specs=pl.BlockSpec(memory_space=pltpu.VMEM),
        scratch_shapes=[
            pltpu.VMEM((requests, each, pairs, width), pages.dtype),
            pltpu.VMEM(out, jnp.float32),
            pltpu.SemaphoreType.DMA((requests,)),
        ],
        compiler_params=pltpu.CompilerParams(vmem_limit_bytes=50 << 20),
        name="attend_pages",
    )(plan, query, pages)


def local(
    queries,
    page_pool,
    page_table,
    serving,
    context_len,
    residual,
    routes,
    route_scores,
    w_gate,
    w_up,
    w_down,
):
    group = ("ep", "sub")
    peers = lax.axis_size(group)
    device = lax.axis_index(group)
    rows_dev, width = residual.shape
    requests_dev = rows_dev // DRAFT
    pages_each = page_table.shape[1]
    pool_pages = page_pool.shape[0]
    listed = requests_dev * pages_each
    fetched = listed // peers
    n_requests = serving.shape[0]

    n_ep = lax.axis_size("ep")
    experts = n_ep // 2
    far, near = peers // 2, peers // 4

    outgoing, packed = stage_pages(
        group,
        page_table.T,
        serving.reshape(1, -1),
        page_pool,
        residual,
        routes.T,
        route_scores.T,
        peers,
        listed,
        experts,
    )
    across = [exchange(packed, group, bit) for bit in (far, far | near, near)]
    pairs = outgoing.shape[1]
    arrived = lax.all_to_all(
        outgoing.reshape(peers, fetched, pairs, 2 * LAT), group, split_axis=0, concat_axis=0, tiled=True
    )

    kept = join_rows([packed, across[0], across[2], across[1]])
    bit = near // 2
    while bit > 1:
        kept = jnp.concatenate([kept, exchange(kept, group, bit)], axis=0)
        bit //= 2
    kept, queries = lax.optimization_barrier((kept, queries))
    other = exchange(kept, group, 1)
    heads = queries.reshape(requests_dev, DRAFT, HEADS, LAT).transpose(0, 2, 1, 3)
    heads = heads.reshape(requests_dev, HEADS * DRAFT, LAT)
    query = jnp.pad(heads, ((0, 0), (0, 0), (0, SHIFT)))
    label = (lax.axis_index("ep") // 2).reshape(1)
    mixed, leaving = expert_rows(label, kept, other, w_gate[0], w_up[0], w_down[0], experts)
    bit = 1
    while True:
        last = exchange(leaving, group, bit)
        bit *= 2
        if bit == peers:
            break
        mixed = mixed + last.astype(jnp.float32)
        if bit == 2:
            mixed, query = lax.optimization_barrier((mixed, query))
        half = mixed.shape[0] // 2
        leaving = mixed[half:].astype(jnp.bfloat16)
        mixed = mixed[:half]

    served = lax.dynamic_slice_in_dim(serving, device * requests_dev, requests_dev)
    slots = jnp.arange(n_requests, dtype=jnp.int32)
    chosen = served[:, None] == slots[None, :]
    own_list = jnp.sum(jnp.where(chosen[:, :, None], page_table[None], 0), axis=1)
    own_list = own_list.reshape(-1) // pool_pages
    position = jnp.arange(listed, dtype=jnp.int32)
    same = (own_list[:, None] == own_list[None, :]) & (position[None, :] < position[:, None])
    place = own_list * fetched + jnp.sum(same.astype(jnp.int32), axis=1)
    limits = jnp.sum(jnp.where(chosen, context_len[None, :], 0), axis=1) - DRAFT
    plan = jnp.concatenate([limits, place])
    latent_out = attend(plan, query, arrived.reshape(listed, pairs, 2 * LAT), pages_each)
    latent_out, last = lax.optimization_barrier((latent_out, last))
    moe_out = (residual.astype(jnp.float32) + mixed + last.astype(jnp.float32)).astype(jnp.bfloat16)
    return (latent_out, moe_out)


def solution(mesh):
    placed = (
        P(("rep", "ep", "sub"), None),
        P(("rep", "ep", "sub"), None),
        P("rep", None),
        P("rep"),
        P("rep"),
        P(("rep", "ep", "sub"), None),
        P(("rep", "ep", "sub"), None),
        P(("rep", "ep", "sub"), None),
        P("ep", None, "sub"),
        P("ep", None, "sub"),
        P("ep", "sub", None),
    )
    return jax.shard_map(
        local,
        mesh=mesh,
        in_specs=placed,
        out_specs=(P(("rep", "ep", "sub"), None), P(("rep", "ep", "sub"), None)),
        check_vma=False,
    )
```

```python
import functools
import math

import jax
import jax.numpy as jnp
from jax import lax
from jax.experimental import pallas as pl
from jax.experimental.pallas import tpu as pltpu
from jax.sharding import PartitionSpec as P

HEADS = 64
LAT = 576
KV = 512
DRAFT = 4
HALF = 640
SHIFT = HALF - LAT

exponent_scale = 192.0 ** (-0.5) * math.log2(math.e)
masked_score = -1e30
PIECES = 4
JOIN_FLOPS = 300_000_000_000
STAGE_FLOPS = 20_000_000_000


def ones_where(condition):
    return jnp.where(condition, 1.0, 0.0).astype(jnp.bfloat16)


def count(left, right):
    return jnp.dot(left, right, preferred_element_type=jnp.float32)


def weigh(routes, scores, experts, lanes):
    top, rows = routes.shape
    scaled = scores / jnp.sum(scores, axis=0, keepdims=True) * 2.5
    labels = lax.broadcasted_iota(jnp.int32, (experts, rows), 0)
    weights = jnp.zeros((experts, rows), jnp.float32)
    for k in range(top):
        weights += jnp.where(labels == routes[k : k + 1, :], scaled[k : k + 1, :], 0.0)
    side = jnp.zeros((rows, lanes), jnp.float32)
    line = lax.broadcasted_iota(jnp.int32, (experts, lanes), 1)
    entry = lax.broadcasted_iota(jnp.int32, (experts, lanes), 0)
    for part in range(3):
        piece = weights.astype(jnp.bfloat16)
        weights = weights - piece.astype(jnp.float32)
        side += lax.dot_general(
            piece,
            ones_where(line == entry + part * experts),
            (((0,), (0,)), ((), ())),
            preferred_element_type=jnp.float32,
        )
    return side.astype(jnp.bfloat16)


def stage_body(peers, group, experts, table_ref, serving_ref, pool_ref, *refs):
    rows_hbm, routes_hbm, scores_hbm, out_ref, packed_ref, *refs = refs
    pool, pages, order, index, table, serving, packed, routes, scores, *sems = refs
    pool_sem, order_sem, table_sems, row_sems, page_sem = sems
    width = rows_hbm.shape[1]
    fetch = pltpu.make_async_copy(pool_ref, pool, pool_sem)
    fetch_table = pltpu.make_async_copy(table_ref, table, table_sems.at[0])
    fetch_serving = pltpu.make_async_copy(serving_ref, serving, table_sems.at[1])
    fetch_rows = [
        pltpu.make_async_copy(routes_hbm, routes, row_sems.at[0]),
        pltpu.make_async_copy(scores_hbm, scores, row_sems.at[1]),
        pltpu.make_async_copy(rows_hbm, packed.at[:, :width], row_sems.at[2]),
    ]
    send_rows = pltpu.make_async_copy(packed, packed_ref, row_sems.at[3])
    fetch_table.start()
    fetch_serving.start()
    for fetch_row in fetch_rows:
        fetch_row.start()
    fetch.start()
    each, slots = table.shape
    span = slots // peers
    fetched = out_ref.shape[0] // peers
    fetch_table.wait()
    fetch_serving.wait()
    held = jnp.full((each, slots), pool.shape[0], jnp.int32)
    listed = table[...]
    named = ones_where(lax.broadcasted_iota(jnp.int32, (slots, slots), 0) == serving[...])
    owner = count(lax.div(listed, held).astype(jnp.float32).astype(jnp.bfloat16), named)
    place = count(lax.rem(listed, held).astype(jnp.float32).astype(jnp.bfloat16), named)
    device = lax.axis_index(group[0]) * lax.axis_size(group[1]) + lax.axis_index(group[1])
    mine = owner == device.astype(jnp.float32)
    flags = ones_where(mine)
    above = lax.broadcasted_iota(jnp.int32, (each, each), 1) < lax.broadcasted_iota(
        jnp.int32, (each, each), 0
    )
    first = lax.broadcasted_iota(jnp.int32, (slots, slots), 0)
    second = lax.broadcasted_iota(jnp.int32, (slots, slots), 1)
    spans = jnp.full((slots, slots), span, jnp.int32)
    before = (lax.div(first, spans) == lax.div(second, spans)) & (first < second)
    whole = jnp.ones((each, each), jnp.bfloat16)
    rank = count(ones_where(above), flags) + count(
        count(whole, flags).astype(jnp.bfloat16), ones_where(before)
    )
    serves = ones_where(
        lax.div(
            lax.broadcasted_iota(jnp.int32, (slots, peers), 0),
            jnp.full((slots, peers), span, jnp.int32),
        )
        == lax.broadcasted_iota(jnp.int32, (slots, peers), 1)
    )
    for k in range(fetched):
        chosen = jnp.where(mine & (rank == k), place, 0.0).astype(jnp.bfloat16)
        column = count(count(whole, chosen).astype(jnp.bfloat16), serves)
        order[k : k + 1, :peers] = column[:1].astype(jnp.int32)
    listing = pltpu.make_async_copy(order, index, order_sem)
    listing.start()
    for fetch_row in fetch_rows:
        fetch_row.wait()
    packed[:, width:] = weigh(routes[...], scores[...], experts, packed.shape[1] - width)
    send_rows.start()
    fetch.wait()
    pages[...] = pool[...].reshape(pages.shape)
    listing.wait()

    def begin(p, carry):
        for k in range(fetched):
            pltpu.make_async_copy(
                pages.at[index[k, p]], out_ref.at[p * fetched + k], page_sem
            ).start()
        return carry

    lax.fori_loop(0, peers, begin, 0, unroll=4)
    send_rows.wait()
    pltpu.make_async_copy(out_ref, out_ref, page_sem).wait()


def stage_pages(group, table, serving, pool, rows, routes, scores, peers, slots, experts):
    side = 3 * experts
    packed = (rows.shape[0], rows.shape[1] + side + -side % 128)
    pairs = pool.shape[1] // (2 * LAT)
    fetched = slots // peers
    listing = (fetched + -fetched % 8, peers + -peers % 128)
    return pl.pallas_call(
        functools.partial(stage_body, peers, group, experts),
        out_shape=(
            jax.ShapeDtypeStruct((slots, pairs, 2 * LAT), pool.dtype),
            jax.ShapeDtypeStruct(packed, rows.dtype),
        ),
        in_specs=[pl.BlockSpec(memory_space=pltpu.HBM)] * 6,
        out_specs=(pl.BlockSpec(memory_space=pltpu.HBM),) * 2,
        scratch_shapes=[
            pltpu.VMEM(pool.shape, pool.dtype),
            pltpu.VMEM((pool.shape[0], pairs, 2 * LAT), pool.dtype),
            pltpu.VMEM(listing, jnp.int32),
            pltpu.SMEM(listing, jnp.int32),
            pltpu.VMEM(table.shape, table.dtype),
            pltpu.VMEM(serving.shape, serving.dtype),
            pltpu.VMEM(packed, rows.dtype),
            pltpu.VMEM(routes.shape, routes.dtype),
            pltpu.VMEM(scores.shape, scores.dtype),
            pltpu.SemaphoreType.DMA,
            pltpu.SemaphoreType.DMA,
            pltpu.SemaphoreType.DMA((2,)),
            pltpu.SemaphoreType.DMA((4,)),
            pltpu.SemaphoreType.DMA,
        ],
        compiler_params=pltpu.CompilerParams(vmem_limit_bytes=56 << 20),
        cost_estimate=pl.CostEstimate(flops=STAGE_FLOPS, bytes_accessed=0, transcendentals=0),
        name="stage_pages",
    )(table, serving, pool, rows, routes, scores)


def join_body(*refs):
    blocks, out_ref = refs[:-1], refs[-1]
    start = 0
    for block_ref in blocks:
        out_ref[start : start + block_ref.shape[0], :] = block_ref[...]
        start += block_ref.shape[0]


def join_rows(blocks):
    rows = sum(block.shape[0] for block in blocks)
    return pl.pallas_call(
        join_body,
        out_shape=jax.ShapeDtypeStruct((rows, blocks[0].shape[1]), blocks[0].dtype),
        cost_estimate=pl.CostEstimate(flops=JOIN_FLOPS, bytes_accessed=0, transcendentals=0),
        name="join_rows",
    )(*blocks)


def exchange(block, group, bit):
    peers = lax.axis_size(group)
    return lax.ppermute(block, group, [(d, d ^ bit) for d in range(peers)])


def expert_body(experts, label_ref, kept_ref, other_ref, *refs):
    gate_hbm, up_hbm, down_hbm, kept_out, other_out, gate_ref, up_ref, down_ref, sems = refs
    copies = [
        pltpu.make_async_copy(gate_hbm, gate_ref, sems.at[0]),
        pltpu.make_async_copy(up_hbm, up_ref, sems.at[1]),
        pltpu.make_async_copy(down_hbm, down_ref, sems.at[2]),
    ]
    for weight_copy in copies:
        weight_copy.start()
    width = gate_ref.shape[0]
    parts = []
    copies[0].wait()
    for rows_ref in (other_ref, kept_ref):
        parts.append(jnp.dot(rows_ref[:, :width], gate_ref[...], preferred_element_type=jnp.float32))
    copies[1].wait()
    hiddens = []
    for rows_ref, gate in zip((other_ref, kept_ref), parts):
        upward = jnp.dot(rows_ref[:, :width], up_ref[...], preferred_element_type=jnp.float32)
        hiddens.append((gate / (1.0 + jnp.exp(-gate)) * upward).astype(jnp.bfloat16))
    copies[2].wait()
    for rows_ref, hidden, out_ref in zip((other_ref, kept_ref), hiddens, (other_out, kept_out)):
        side = rows_ref[:, width:].astype(jnp.float32)
        line = lax.broadcasted_iota(jnp.int32, side.shape, 1)
        mine = (line == label_ref[0]) | (line == label_ref[0] + experts)
        mine = mine | (line == label_ref[0] + 2 * experts)
        weight = jnp.sum(jnp.where(mine, side, 0.0), axis=1, keepdims=True)
        total = jnp.dot(hidden, down_ref[...], preferred_element_type=jnp.float32) * weight
        out_ref[...] = total.astype(out_ref.dtype)


def expert_rows(label, kept, other, gate, up, down, experts):
    return pl.pallas_call(
        functools.partial(expert_body, experts),
        out_shape=(
            jax.ShapeDtypeStruct((kept.shape[0], gate.shape[0]), jnp.float32),
            jax.ShapeDtypeStruct((other.shape[0], gate.shape[0]), jnp.bfloat16),
        ),
        in_specs=[pl.BlockSpec(memory_space=pltpu.SMEM)]
        + [pl.BlockSpec(memory_space=pltpu.VMEM)] * 2
        + [pl.BlockSpec(memory_space=pltpu.HBM)] * 3,
        scratch_shapes=[
            pltpu.VMEM(gate.shape, gate.dtype),
            pltpu.VMEM(up.shape, up.dtype),
            pltpu.VMEM(down.shape, down.dtype),
            pltpu.SemaphoreType.DMA((3,)),
        ],
        compiler_params=pltpu.CompilerParams(vmem_limit_bytes=56 << 20),
        cost_estimate=pl.CostEstimate(flops=0, bytes_accessed=0, transcendentals=0),
        name="expert_rows",
    )(label, kept, other, gate, up, down)


def attend_body(plan_ref, query_ref, pages_ref, out_ref, context, held, packed, sems, out_sem):
    requests, each, pairs, width = context.shape
    rows = query_ref.shape[1]
    contract = (((1,), (1,)), ((), ()))

    for r in range(requests):

        def begin(i, carry, r=r):
            pltpu.make_async_copy(
                pages_ref.at[plan_ref[requests + r * each + i]], context.at[r, i], sems.at[r]
            ).start()
            return carry

        lax.fori_loop(0, each, begin, 0, unroll=4)

    columns = each * pairs
    draft = lax.broadcasted_iota(jnp.int32, (rows, columns), 0) % DRAFT
    early = 2 * lax.broadcasted_iota(jnp.int32, (rows, columns), 1) - draft

    def score(r):
        pltpu.make_async_copy(context.at[r], context.at[r], sems.at[r]).wait()
        block = context[r].reshape(columns, width)
        low = query_ref[r]
        high = pltpu.roll(low.astype(jnp.float32), SHIFT, 1).astype(low.dtype)
        even = lax.dot_general(
            low, block[:, :HALF], contract, preferred_element_type=jnp.float32
        )
        odd = lax.dot_general(
            high, block[:, width - HALF :], contract, preferred_element_type=jnp.float32
        )
        return even, odd

    scored = score(0)
    for r in range(requests):
        even, odd = scored
        if r + 1 < requests:
            scored = score(r + 1)
        limit = plan_ref[r]
        even = jnp.where(early <= limit, even, masked_score)
        odd = jnp.where(early < limit, odd, masked_score)
        highest = jnp.max(jnp.maximum(even, odd), axis=-1, keepdims=True)
        even = jnp.exp2((even - highest) * exponent_scale)
        odd = jnp.exp2((odd - highest) * exponent_scale)
        total = jnp.sum(even + odd, axis=-1, keepdims=True)
        block = context[r].reshape(columns, width)
        latent = jnp.dot(
            even.astype(jnp.bfloat16), block[:, :KV], preferred_element_type=jnp.float32
        )
        other = jnp.dot(
            odd.astype(jnp.bfloat16), block[:, width - HALF :], preferred_element_type=jnp.float32
        )
        latent = (latent + other[:, SHIFT : SHIFT + KV]) * (1.0 / total)
        for h in range(rows // DRAFT):
            held[r * DRAFT : (r + 1) * DRAFT, h * KV : (h + 1) * KV] = latent[
                h * DRAFT : (h + 1) * DRAFT, :
            ]
    span = held.shape[1] // PIECES
    for piece in range(PIECES):
        lanes = slice(piece * span, (piece + 1) * span)
        packed[:, lanes] = held[:, lanes].astype(packed.dtype)
        pltpu.make_async_copy(packed.at[:, lanes], out_ref.at[:, lanes], out_sem).start()
    pltpu.make_async_copy(packed, out_ref, out_sem).wait()


def attend(plan, query, pages, each):
    requests, rows, _ = query.shape
    _, pairs, width = pages.shape
    out = (requests * DRAFT, (rows // DRAFT) * KV)
    return pl.pallas_call(
        attend_body,
        out_shape=jax.ShapeDtypeStruct(out, jnp.bfloat16),
        in_specs=[
            pl.BlockSpec(memory_space=pltpu.SMEM),
            pl.BlockSpec(memory_space=pltpu.VMEM),
            pl.BlockSpec(memory_space=pltpu.HBM),
        ],
        out_specs=pl.BlockSpec(memory_space=pltpu.HBM),
        scratch_shapes=[
            pltpu.VMEM((requests, each, pairs, width), pages.dtype),
            pltpu.VMEM(out, jnp.float32),
            pltpu.VMEM(out, jnp.bfloat16),
            pltpu.SemaphoreType.DMA((requests,)),
            pltpu.SemaphoreType.DMA,
        ],
        compiler_params=pltpu.CompilerParams(vmem_limit_bytes=50 << 20),
        name="attend_pages",
    )(plan, query, pages)


def local(
    queries,
    page_pool,
    page_table,
    serving,
    context_len,
    residual,
    routes,
    route_scores,
    w_gate,
    w_up,
    w_down,
):
    group = ("ep", "sub")
    peers = lax.axis_size(group)
    device = lax.axis_index(group)
    rows_dev, width = residual.shape
    requests_dev = rows_dev // DRAFT
    pages_each = page_table.shape[1]
    pool_pages = page_pool.shape[0]
    listed = requests_dev * pages_each
    fetched = listed // peers
    n_requests = serving.shape[0]

    n_ep = lax.axis_size("ep")
    experts = n_ep // 2
    far, near = peers // 2, peers // 4

    outgoing, packed = stage_pages(
        group,
        page_table.T,
        serving.reshape(1, -1),
        page_pool,
        residual,
        routes.T,
        route_scores.T,
        peers,
        listed,
        experts,
    )
    across = [exchange(packed, group, bit) for bit in (far, far | near, near)]
    pairs = outgoing.shape[1]
    arrived = lax.all_to_all(
        outgoing.reshape(peers, fetched, pairs, 2 * LAT), group, split_axis=0, concat_axis=0, tiled=True
    )

    kept = join_rows([packed, across[0], across[2], across[1]])
    bit = near // 2
    while bit > 1:
        kept = jnp.concatenate([kept, exchange(kept, group, bit)], axis=0)
        bit //= 2
    kept, queries = lax.optimization_barrier((kept, queries))
    other = exchange(kept, group, 1)
    heads = queries.reshape(requests_dev, DRAFT, HEADS, LAT).transpose(0, 2, 1, 3)
    heads = heads.reshape(requests_dev, HEADS * DRAFT, LAT)
    query = jnp.pad(heads, ((0, 0), (0, 0), (0, SHIFT)))
    label = (lax.axis_index("ep") // 2).reshape(1)
    mixed, leaving = expert_rows(label, kept, other, w_gate[0], w_up[0], w_down[0], experts)
    bit = 1
    while True:
        last = exchange(leaving, group, bit)
        bit *= 2
        if bit == peers:
            break
        mixed = mixed + last.astype(jnp.float32)
        if bit == 2:
            mixed, query = lax.optimization_barrier((mixed, query))
        half = mixed.shape[0] // 2
        leaving = mixed[half:].astype(jnp.bfloat16)
        mixed = mixed[:half]

    served = lax.dynamic_slice_in_dim(serving, device * requests_dev, requests_dev)
    slots = jnp.arange(n_requests, dtype=jnp.int32)
    chosen = served[:, None] == slots[None, :]
    own_list = jnp.sum(jnp.where(chosen[:, :, None], page_table[None], 0), axis=1)
    own_list = own_list.reshape(-1) // pool_pages
    position = jnp.arange(listed, dtype=jnp.int32)
    same = (own_list[:, None] == own_list[None, :]) & (position[None, :] < position[:, None])
    place = own_list * fetched + jnp.sum(same.astype(jnp.int32), axis=1)
    limits = jnp.sum(jnp.where(chosen, context_len[None, :], 0), axis=1) - DRAFT
    plan = jnp.concatenate([limits, place])
    latent_out = attend(plan, query, arrived.reshape(listed, pairs, 2 * LAT), pages_each)
    latent_out, last = lax.optimization_barrier((latent_out, last))
    moe_out = (residual.astype(jnp.float32) + mixed + last.astype(jnp.float32)).astype(jnp.bfloat16)
    return (latent_out, moe_out)


def solution(mesh):
    placed = (
        P(("rep", "ep", "sub"), None),
        P(("rep", "ep", "sub"), None),
        P("rep", None),
        P("rep"),
        P("rep"),
        P(("rep", "ep", "sub"), None),
        P(("rep", "ep", "sub"), None),
        P(("rep", "ep", "sub"), None),
        P("ep", None, "sub"),
        P("ep", None, "sub"),
        P("ep", "sub", None),
    )
    return jax.shard_map(
        local,
        mesh=mesh,
        in_specs=placed,
        out_specs=(P(("rep", "ep", "sub"), None), P(("rep", "ep", "sub"), None)),
        check_vma=False,
    )
```

```python
import functools
import math

import jax
import jax.numpy as jnp
from jax import lax
from jax.experimental import pallas as pl
from jax.experimental.pallas import tpu as pltpu
from jax.sharding import PartitionSpec as P

HEADS = 64
LAT = 576
KV = 512
DRAFT = 4
HALF = 640
SHIFT = HALF - LAT

exponent_scale = 192.0 ** (-0.5) * math.log2(math.e)
masked_score = -1e30
PIECES = 4
JOIN_FLOPS = 300_000_000_000
STAGE_FLOPS = 20_000_000_000


def ones_where(condition):
    return jnp.where(condition, 1.0, 0.0).astype(jnp.bfloat16)


def count(left, right):
    return jnp.dot(left, right, preferred_element_type=jnp.float32)


def weigh(routes, scores, experts, lanes):
    top, rows = routes.shape
    scaled = scores / jnp.sum(scores, axis=0, keepdims=True) * 2.5
    labels = lax.broadcasted_iota(jnp.int32, (experts, rows), 0)
    weights = jnp.zeros((experts, rows), jnp.float32)
    for k in range(top):
        weights += jnp.where(labels == routes[k : k + 1, :], scaled[k : k + 1, :], 0.0)
    side = jnp.zeros((rows, lanes), jnp.float32)
    line = lax.broadcasted_iota(jnp.int32, (experts, lanes), 1)
    entry = lax.broadcasted_iota(jnp.int32, (experts, lanes), 0)
    for part in range(3):
        piece = weights.astype(jnp.bfloat16)
        weights = weights - piece.astype(jnp.float32)
        side += lax.dot_general(
            piece,
            ones_where(line == entry + part * experts),
            (((0,), (0,)), ((), ())),
            preferred_element_type=jnp.float32,
        )
    return side.astype(jnp.bfloat16)


def stage_body(peers, group, experts, table_ref, serving_ref, pool_ref, *refs):
    rows_hbm, routes_hbm, scores_hbm, out_ref, packed_ref, *refs = refs
    pool, pages, order, index, table, serving, packed, routes, scores, *sems = refs
    pool_sem, order_sem, table_sems, row_sems, page_sem = sems
    width = rows_hbm.shape[1]
    fetch = pltpu.make_async_copy(pool_ref, pool, pool_sem)
    fetch_table = pltpu.make_async_copy(table_ref, table, table_sems.at[0])
    fetch_serving = pltpu.make_async_copy(serving_ref, serving, table_sems.at[1])
    fetch_rows = [
        pltpu.make_async_copy(routes_hbm, routes, row_sems.at[0]),
        pltpu.make_async_copy(scores_hbm, scores, row_sems.at[1]),
        pltpu.make_async_copy(rows_hbm, packed.at[:, :width], row_sems.at[2]),
    ]
    send_rows = pltpu.make_async_copy(packed, packed_ref, row_sems.at[3])
    fetch_table.start()
    fetch_serving.start()
    fetch.start()
    for fetch_row in fetch_rows:
        fetch_row.start()
    each, slots = table.shape
    span = slots // peers
    fetched = out_ref.shape[0] // peers
    fetch_table.wait()
    fetch_serving.wait()
    held = jnp.full((each, slots), pool.shape[0], jnp.int32)
    listed = table[...]
    named = ones_where(lax.broadcasted_iota(jnp.int32, (slots, slots), 0) == serving[...])
    owner = count(lax.div(listed, held).astype(jnp.float32).astype(jnp.bfloat16), named)
    place = count(lax.rem(listed, held).astype(jnp.float32).astype(jnp.bfloat16), named)
    device = lax.axis_index(group[0]) * lax.axis_size(group[1]) + lax.axis_index(group[1])
    mine = owner == device.astype(jnp.float32)
    flags = ones_where(mine)
    above = lax.broadcasted_iota(jnp.int32, (each, each), 1) < lax.broadcasted_iota(
        jnp.int32, (each, each), 0
    )
    first = lax.broadcasted_iota(jnp.int32, (slots, slots), 0)
    second = lax.broadcasted_iota(jnp.int32, (slots, slots), 1)
    spans = jnp.full((slots, slots), span, jnp.int32)
    before = (lax.div(first, spans) == lax.div(second, spans)) & (first < second)
    whole = jnp.ones((each, each), jnp.bfloat16)
    rank = count(ones_where(above), flags) + count(
        count(whole, flags).astype(jnp.bfloat16), ones_where(before)
    )
    serves = ones_where(
        lax.div(
            lax.broadcasted_iota(jnp.int32, (slots, peers), 0),
            jnp.full((slots, peers), span, jnp.int32),
        )
        == lax.broadcasted_iota(jnp.int32, (slots, peers), 1)
    )
    for k in range(fetched):
        chosen = jnp.where(mine & (rank == k), place, 0.0).astype(jnp.bfloat16)
        column = count(count(whole, chosen).astype(jnp.bfloat16), serves)
        order[k : k + 1, :peers] = column[:1].astype(jnp.int32)
    listing = pltpu.make_async_copy(order, index, order_sem)
    listing.start()
    for fetch_row in fetch_rows:
        fetch_row.wait()
    packed[:, width:] = weigh(routes[...], scores[...], experts, packed.shape[1] - width)
    send_rows.start()
    fetch.wait()
    pages[...] = pool[...].reshape(pages.shape)
    listing.wait()

    def begin(p, carry):
        for k in range(fetched):
            pltpu.make_async_copy(
                pages.at[index[k, p]], out_ref.at[p * fetched + k], page_sem
            ).start()
        return carry

    lax.fori_loop(0, peers, begin, 0, unroll=4)
    send_rows.wait()
    pltpu.make_async_copy(out_ref, out_ref, page_sem).wait()


def stage_pages(group, table, serving, pool, rows, routes, scores, peers, slots, experts):
    side = 3 * experts
    packed = (rows.shape[0], rows.shape[1] + side + -side % 128)
    pairs = pool.shape[1] // (2 * LAT)
    fetched = slots // peers
    listing = (fetched + -fetched % 8, peers + -peers % 128)
    return pl.pallas_call(
        functools.partial(stage_body, peers, group, experts),
        out_shape=(
            jax.ShapeDtypeStruct((slots, pairs, 2 * LAT), pool.dtype),
            jax.ShapeDtypeStruct(packed, rows.dtype),
        ),
        in_specs=[pl.BlockSpec(memory_space=pltpu.HBM)] * 6,
        out_specs=(pl.BlockSpec(memory_space=pltpu.HBM),) * 2,
        scratch_shapes=[
            pltpu.VMEM(pool.shape, pool.dtype),
            pltpu.VMEM((pool.shape[0], pairs, 2 * LAT), pool.dtype),
            pltpu.VMEM(listing, jnp.int32),
            pltpu.SMEM(listing, jnp.int32),
            pltpu.VMEM(table.shape, table.dtype),
            pltpu.VMEM(serving.shape, serving.dtype),
            pltpu.VMEM(packed, rows.dtype),
            pltpu.VMEM(routes.shape, routes.dtype),
            pltpu.VMEM(scores.shape, scores.dtype),
            pltpu.SemaphoreType.DMA,
            pltpu.SemaphoreType.DMA,
            pltpu.SemaphoreType.DMA((2,)),
            pltpu.SemaphoreType.DMA((4,)),
            pltpu.SemaphoreType.DMA,
        ],
        compiler_params=pltpu.CompilerParams(vmem_limit_bytes=56 << 20),
        cost_estimate=pl.CostEstimate(flops=STAGE_FLOPS, bytes_accessed=0, transcendentals=0),
        name="stage_pages",
    )(table, serving, pool, rows, routes, scores)


def join_body(*refs):
    blocks, out_ref = refs[:-1], refs[-1]
    start = 0
    for block_ref in blocks:
        out_ref[start : start + block_ref.shape[0], :] = block_ref[...]
        start += block_ref.shape[0]


def join_rows(blocks):
    rows = sum(block.shape[0] for block in blocks)
    return pl.pallas_call(
        join_body,
        out_shape=jax.ShapeDtypeStruct((rows, blocks[0].shape[1]), blocks[0].dtype),
        cost_estimate=pl.CostEstimate(flops=JOIN_FLOPS, bytes_accessed=0, transcendentals=0),
        name="join_rows",
    )(*blocks)


def exchange(block, group, bit):
    peers = lax.axis_size(group)
    return lax.ppermute(block, group, [(d, d ^ bit) for d in range(peers)])


def expert_body(experts, label_ref, kept_ref, other_ref, *refs):
    gate_hbm, up_hbm, down_hbm, kept_out, other_out, gate_ref, up_ref, down_ref, sems = refs
    copies = [
        pltpu.make_async_copy(gate_hbm, gate_ref, sems.at[0]),
        pltpu.make_async_copy(up_hbm, up_ref, sems.at[1]),
        pltpu.make_async_copy(down_hbm, down_ref, sems.at[2]),
    ]
    for weight_copy in copies:
        weight_copy.start()
    width = gate_ref.shape[0]
    parts = []
    copies[0].wait()
    for rows_ref in (other_ref, kept_ref):
        parts.append(jnp.dot(rows_ref[:, :width], gate_ref[...], preferred_element_type=jnp.float32))
    copies[1].wait()
    hiddens = []
    for rows_ref, gate in zip((other_ref, kept_ref), parts):
        upward = jnp.dot(rows_ref[:, :width], up_ref[...], preferred_element_type=jnp.float32)
        hiddens.append((gate / (1.0 + jnp.exp(-gate)) * upward).astype(jnp.bfloat16))
    copies[2].wait()
    for rows_ref, hidden, out_ref in zip((other_ref, kept_ref), hiddens, (other_out, kept_out)):
        side = rows_ref[:, width:].astype(jnp.float32)
        line = lax.broadcasted_iota(jnp.int32, side.shape, 1)
        mine = (line == label_ref[0]) | (line == label_ref[0] + experts)
        mine = mine | (line == label_ref[0] + 2 * experts)
        weight = jnp.sum(jnp.where(mine, side, 0.0), axis=1, keepdims=True)
        total = jnp.dot(hidden, down_ref[...], preferred_element_type=jnp.float32) * weight
        out_ref[...] = total.astype(out_ref.dtype)


def expert_rows(label, kept, other, gate, up, down, experts):
    return pl.pallas_call(
        functools.partial(expert_body, experts),
        out_shape=(
            jax.ShapeDtypeStruct((kept.shape[0], gate.shape[0]), jnp.float32),
            jax.ShapeDtypeStruct((other.shape[0], gate.shape[0]), jnp.bfloat16),
        ),
        in_specs=[pl.BlockSpec(memory_space=pltpu.SMEM)]
        + [pl.BlockSpec(memory_space=pltpu.VMEM)] * 2
        + [pl.BlockSpec(memory_space=pltpu.HBM)] * 3,
        scratch_shapes=[
            pltpu.VMEM(gate.shape, gate.dtype),
            pltpu.VMEM(up.shape, up.dtype),
            pltpu.VMEM(down.shape, down.dtype),
            pltpu.SemaphoreType.DMA((3,)),
        ],
        compiler_params=pltpu.CompilerParams(vmem_limit_bytes=56 << 20),
        cost_estimate=pl.CostEstimate(flops=0, bytes_accessed=0, transcendentals=0),
        name="expert_rows",
    )(label, kept, other, gate, up, down)


def attend_body(plan_ref, query_ref, high_ref, pages_ref, out_ref, context, held, packed, sems, out_sem):
    requests, each, pairs, width = context.shape
    rows = query_ref.shape[1]
    contract = (((1,), (1,)), ((), ()))

    for r in range(requests):

        def begin(i, carry, r=r):
            pltpu.make_async_copy(
                pages_ref.at[plan_ref[requests + r * each + i]], context.at[r, i], sems.at[r]
            ).start()
            return carry

        lax.fori_loop(0, each, begin, 0, unroll=4)

    columns = each * pairs
    draft = lax.broadcasted_iota(jnp.int32, (rows, columns), 0) % DRAFT
    early = 2 * lax.broadcasted_iota(jnp.int32, (rows, columns), 1) - draft

    def score(r):
        pltpu.make_async_copy(context.at[r], context.at[r], sems.at[r]).wait()
        block = context[r].reshape(columns, width)
        low = query_ref[r]
        high = high_ref[r]
        even = lax.dot_general(
            low, block[:, :HALF], contract, preferred_element_type=jnp.float32
        )
        odd = lax.dot_general(
            high, block[:, width - HALF :], contract, preferred_element_type=jnp.float32
        )
        return even, odd

    scored = score(0)
    for r in range(requests):
        even, odd = scored
        if r + 1 < requests:
            scored = score(r + 1)
        limit = plan_ref[r]
        even = jnp.where(early <= limit, even, masked_score)
        odd = jnp.where(early < limit, odd, masked_score)
        highest = jnp.max(jnp.maximum(even, odd), axis=-1, keepdims=True)
        even = jnp.exp2((even - highest) * exponent_scale)
        odd = jnp.exp2((odd - highest) * exponent_scale)
        total = jnp.sum(even + odd, axis=-1, keepdims=True)
        block = context[r].reshape(columns, width)
        latent = jnp.dot(
            even.astype(jnp.bfloat16), block[:, :KV], preferred_element_type=jnp.float32
        )
        other = jnp.dot(
            odd.astype(jnp.bfloat16), block[:, width - HALF :], preferred_element_type=jnp.float32
        )
        latent = (latent + other[:, SHIFT : SHIFT + KV]) * (1.0 / total)
        for h in range(rows // DRAFT):
            held[r * DRAFT : (r + 1) * DRAFT, h * KV : (h + 1) * KV] = latent[
                h * DRAFT : (h + 1) * DRAFT, :
            ]
    span = held.shape[1] // PIECES
    for piece in range(PIECES):
        lanes = slice(piece * span, (piece + 1) * span)
        packed[:, lanes] = held[:, lanes].astype(packed.dtype)
        pltpu.make_async_copy(packed.at[:, lanes], out_ref.at[:, lanes], out_sem).start()
    pltpu.make_async_copy(packed, out_ref, out_sem).wait()


def attend(plan, query, high, pages, each):
    requests, rows, _ = query.shape
    _, pairs, width = pages.shape
    out = (requests * DRAFT, (rows // DRAFT) * KV)
    return pl.pallas_call(
        attend_body,
        out_shape=jax.ShapeDtypeStruct(out, jnp.bfloat16),
        in_specs=[
            pl.BlockSpec(memory_space=pltpu.SMEM),
            pl.BlockSpec(memory_space=pltpu.VMEM),
            pl.BlockSpec(memory_space=pltpu.VMEM),
            pl.BlockSpec(memory_space=pltpu.HBM),
        ],
        out_specs=pl.BlockSpec(memory_space=pltpu.HBM),
        scratch_shapes=[
            pltpu.VMEM((requests, each, pairs, width), pages.dtype),
            pltpu.VMEM(out, jnp.float32),
            pltpu.VMEM(out, jnp.bfloat16),
            pltpu.SemaphoreType.DMA((requests,)),
            pltpu.SemaphoreType.DMA,
        ],
        compiler_params=pltpu.CompilerParams(vmem_limit_bytes=50 << 20),
        name="attend_pages",
    )(plan, query, high, pages)


def local(
    queries,
    page_pool,
    page_table,
    serving,
    context_len,
    residual,
    routes,
    route_scores,
    w_gate,
    w_up,
    w_down,
):
    group = ("ep", "sub")
    peers = lax.axis_size(group)
    device = lax.axis_index(group)
    rows_dev, width = residual.shape
    requests_dev = rows_dev // DRAFT
    pages_each = page_table.shape[1]
    pool_pages = page_pool.shape[0]
    listed = requests_dev * pages_each
    fetched = listed // peers
    n_requests = serving.shape[0]

    n_ep = lax.axis_size("ep")
    experts = n_ep // 2
    far, near = peers // 2, peers // 4

    outgoing, packed = stage_pages(
        group,
        page_table.T,
        serving.reshape(1, -1),
        page_pool,
        residual,
        routes.T,
        route_scores.T,
        peers,
        listed,
        experts,
    )
    across = [exchange(packed, group, bit) for bit in (far, far | near, near)]
    pairs = outgoing.shape[1]
    arrived = lax.all_to_all(
        outgoing.reshape(peers, fetched, pairs, 2 * LAT), group, split_axis=0, concat_axis=0, tiled=True
    )

    kept = join_rows([packed, across[0], across[2], across[1]])
    bit = near // 2
    while bit > 1:
        kept = jnp.concatenate([kept, exchange(kept, group, bit)], axis=0)
        bit //= 2
    kept, queries = lax.optimization_barrier((kept, queries))
    other = exchange(kept, group, 1)
    heads = queries.reshape(requests_dev, DRAFT, HEADS, LAT).transpose(0, 2, 1, 3)
    heads = heads.reshape(requests_dev, HEADS * DRAFT, LAT)
    query = [jnp.pad(heads, ((0, 0), (0, 0), sides)) for sides in ((0, SHIFT), (SHIFT, 0))]
    label = (lax.axis_index("ep") // 2).reshape(1)
    mixed, leaving = expert_rows(label, kept, other, w_gate[0], w_up[0], w_down[0], experts)
    bit = 1
    while True:
        last = exchange(leaving, group, bit)
        bit *= 2
        if bit == peers:
            break
        mixed = mixed + last.astype(jnp.float32)
        if bit == 2:
            mixed, query = lax.optimization_barrier((mixed, query))
        half = mixed.shape[0] // 2
        leaving = mixed[half:].astype(jnp.bfloat16)
        mixed = mixed[:half]

    served = lax.dynamic_slice_in_dim(serving, device * requests_dev, requests_dev)
    slots = jnp.arange(n_requests, dtype=jnp.int32)
    chosen = served[:, None] == slots[None, :]
    own_list = jnp.sum(jnp.where(chosen[:, :, None], page_table[None], 0), axis=1)
    own_list = own_list.reshape(-1) // pool_pages
    position = jnp.arange(listed, dtype=jnp.int32)
    same = (own_list[:, None] == own_list[None, :]) & (position[None, :] < position[:, None])
    place = own_list * fetched + jnp.sum(same.astype(jnp.int32), axis=1)
    limits = jnp.sum(jnp.where(chosen, context_len[None, :], 0), axis=1) - DRAFT
    plan = jnp.concatenate([limits, place])
    latent_out = attend(plan, *query, arrived.reshape(listed, pairs, 2 * LAT), pages_each)
    latent_out, last = lax.optimization_barrier((latent_out, last))
    moe_out = (residual.astype(jnp.float32) + mixed + last.astype(jnp.float32)).astype(jnp.bfloat16)
    return (latent_out, moe_out)


def solution(mesh):
    placed = (
        P(("rep", "ep", "sub"), None),
        P(("rep", "ep", "sub"), None),
        P("rep", None),
        P("rep"),
        P("rep"),
        P(("rep", "ep", "sub"), None),
        P(("rep", "ep", "sub"), None),
        P(("rep", "ep", "sub"), None),
        P("ep", None, "sub"),
        P("ep", None, "sub"),
        P("ep", "sub", None),
    )
    return jax.shard_map(
        local,
        mesh=mesh,
        in_specs=placed,
        out_specs=(P(("rep", "ep", "sub"), None), P(("rep", "ep", "sub"), None)),
        check_vma=False,
    )
```

```python
import functools
import math

import jax
import jax.numpy as jnp
from jax import lax
from jax.experimental import pallas as pl
from jax.experimental.pallas import tpu as pltpu
from jax.sharding import PartitionSpec as P

HEADS = 64
LAT = 576
KV = 512
DRAFT = 4
HALF = 640
SHIFT = HALF - LAT

exponent_scale = 192.0 ** (-0.5) * math.log2(math.e)
masked_score = -1e30
PIECES = 4
JOIN_FLOPS = 300_000_000_000
STAGE_FLOPS = 20_000_000_000


def ones_where(condition):
    return jnp.where(condition, 1.0, 0.0).astype(jnp.bfloat16)


def count(left, right):
    return jnp.dot(left, right, preferred_element_type=jnp.float32)


def weigh(routes, scores, experts, lanes):
    top, rows = routes.shape
    scaled = scores / jnp.sum(scores, axis=0, keepdims=True) * 2.5
    labels = lax.broadcasted_iota(jnp.int32, (experts, rows), 0)
    weights = jnp.zeros((experts, rows), jnp.float32)
    for k in range(top):
        weights += jnp.where(labels == routes[k : k + 1, :], scaled[k : k + 1, :], 0.0)
    side = jnp.zeros((rows, lanes), jnp.float32)
    line = lax.broadcasted_iota(jnp.int32, (experts, lanes), 1)
    entry = lax.broadcasted_iota(jnp.int32, (experts, lanes), 0)
    for part in range(3):
        piece = weights.astype(jnp.bfloat16)
        weights = weights - piece.astype(jnp.float32)
        side += lax.dot_general(
            piece,
            ones_where(line == entry + part * experts),
            (((0,), (0,)), ((), ())),
            preferred_element_type=jnp.float32,
        )
    return side.astype(jnp.bfloat16)


def stage_body(peers, group, experts, table_ref, serving_ref, pool_ref, *refs):
    rows_hbm, routes_hbm, scores_hbm, out_ref, packed_ref, *refs = refs
    pool, pages, order, index, table, serving, packed, routes, scores, *sems = refs
    pool_sem, order_sem, table_sems, row_sems, page_sem = sems
    width = rows_hbm.shape[1]
    fetch = pltpu.make_async_copy(pool_ref, pool, pool_sem)
    fetch_table = pltpu.make_async_copy(table_ref, table, table_sems.at[0])
    fetch_serving = pltpu.make_async_copy(serving_ref, serving, table_sems.at[1])
    fetch_rows = [
        pltpu.make_async_copy(routes_hbm, routes, row_sems.at[0]),
        pltpu.make_async_copy(scores_hbm, scores, row_sems.at[1]),
        pltpu.make_async_copy(rows_hbm, packed.at[:, :width], row_sems.at[2]),
    ]
    send_rows = pltpu.make_async_copy(packed, packed_ref, row_sems.at[3])
    fetch_table.start()
    fetch_serving.start()
    fetch.start()
    for fetch_row in fetch_rows:
        fetch_row.start()
    each, slots = table.shape
    span = slots // peers
    fetched = out_ref.shape[0] // peers
    fetch_table.wait()
    fetch_serving.wait()
    held = jnp.full((each, slots), pool.shape[0], jnp.int32)
    listed = table[...]
    named = ones_where(lax.broadcasted_iota(jnp.int32, (slots, slots), 0) == serving[...])
    owner = count(lax.div(listed, held).astype(jnp.float32).astype(jnp.bfloat16), named)
    place = count(lax.rem(listed, held).astype(jnp.float32).astype(jnp.bfloat16), named)
    device = lax.axis_index(group[0]) * lax.axis_size(group[1]) + lax.axis_index(group[1])
    mine = owner == device.astype(jnp.float32)
    flags = ones_where(mine)
    above = lax.broadcasted_iota(jnp.int32, (each, each), 1) < lax.broadcasted_iota(
        jnp.int32, (each, each), 0
    )
    first = lax.broadcasted_iota(jnp.int32, (slots, slots), 0)
    second = lax.broadcasted_iota(jnp.int32, (slots, slots), 1)
    spans = jnp.full((slots, slots), span, jnp.int32)
    before = (lax.div(first, spans) == lax.div(second, spans)) & (first < second)
    whole = jnp.ones((each, each), jnp.bfloat16)
    rank = count(ones_where(above), flags) + count(
        count(whole, flags).astype(jnp.bfloat16), ones_where(before)
    )
    serves = ones_where(
        lax.div(
            lax.broadcasted_iota(jnp.int32, (slots, peers), 0),
            jnp.full((slots, peers), span, jnp.int32),
        )
        == lax.broadcasted_iota(jnp.int32, (slots, peers), 1)
    )
    for k in range(fetched):
        chosen = jnp.where(mine & (rank == k), place, 0.0).astype(jnp.bfloat16)
        column = count(count(whole, chosen).astype(jnp.bfloat16), serves)
        order[k : k + 1, :peers] = column[:1].astype(jnp.int32)
    listing = pltpu.make_async_copy(order, index, order_sem)
    listing.start()
    for fetch_row in fetch_rows:
        fetch_row.wait()
    packed[:, width:] = weigh(routes[...], scores[...], experts, packed.shape[1] - width)
    send_rows.start()
    fetch.wait()
    pages[...] = pool[...].reshape(pages.shape)
    listing.wait()

    def begin(p, carry):
        for k in range(fetched):
            pltpu.make_async_copy(
                pages.at[index[k, p]], out_ref.at[p * fetched + k], page_sem
            ).start()
        return carry

    lax.fori_loop(0, peers, begin, 0, unroll=4)
    send_rows.wait()
    pltpu.make_async_copy(out_ref, out_ref, page_sem).wait()


def stage_pages(group, table, serving, pool, rows, routes, scores, peers, slots, experts):
    side = 3 * experts
    packed = (rows.shape[0], rows.shape[1] + side + -side % 128)
    pairs = pool.shape[1] // (2 * LAT)
    fetched = slots // peers
    listing = (fetched + -fetched % 8, peers + -peers % 128)
    return pl.pallas_call(
        functools.partial(stage_body, peers, group, experts),
        out_shape=(
            jax.ShapeDtypeStruct((slots, pairs, 2 * LAT), pool.dtype),
            jax.ShapeDtypeStruct(packed, rows.dtype),
        ),
        in_specs=[pl.BlockSpec(memory_space=pltpu.HBM)] * 6,
        out_specs=(pl.BlockSpec(memory_space=pltpu.HBM),) * 2,
        scratch_shapes=[
            pltpu.VMEM(pool.shape, pool.dtype),
            pltpu.VMEM((pool.shape[0], pairs, 2 * LAT), pool.dtype),
            pltpu.VMEM(listing, jnp.int32),
            pltpu.SMEM(listing, jnp.int32),
            pltpu.VMEM(table.shape, table.dtype),
            pltpu.VMEM(serving.shape, serving.dtype),
            pltpu.VMEM(packed, rows.dtype),
            pltpu.VMEM(routes.shape, routes.dtype),
            pltpu.VMEM(scores.shape, scores.dtype),
            pltpu.SemaphoreType.DMA,
            pltpu.SemaphoreType.DMA,
            pltpu.SemaphoreType.DMA((2,)),
            pltpu.SemaphoreType.DMA((4,)),
            pltpu.SemaphoreType.DMA,
        ],
        compiler_params=pltpu.CompilerParams(vmem_limit_bytes=56 << 20),
        cost_estimate=pl.CostEstimate(flops=STAGE_FLOPS, bytes_accessed=0, transcendentals=0),
        name="stage_pages",
    )(table, serving, pool, rows, routes, scores)


def join_body(*refs):
    blocks, out_ref = refs[:-1], refs[-1]
    start = 0
    for block_ref in blocks:
        out_ref[start : start + block_ref.shape[0], :] = block_ref[...]
        start += block_ref.shape[0]


def join_rows(blocks):
    rows = sum(block.shape[0] for block in blocks)
    return pl.pallas_call(
        join_body,
        out_shape=jax.ShapeDtypeStruct((rows, blocks[0].shape[1]), blocks[0].dtype),
        cost_estimate=pl.CostEstimate(flops=JOIN_FLOPS, bytes_accessed=0, transcendentals=0),
        name="join_rows",
    )(*blocks)


def exchange(block, group, bit):
    peers = lax.axis_size(group)
    return lax.ppermute(block, group, [(d, d ^ bit) for d in range(peers)])


def expert_body(experts, label_ref, kept_ref, other_ref, *refs):
    gate_hbm, up_hbm, down_hbm, kept_out, other_out, gate_ref, up_ref, down_ref, sems = refs
    copies = [
        pltpu.make_async_copy(gate_hbm, gate_ref, sems.at[0]),
        pltpu.make_async_copy(up_hbm, up_ref, sems.at[1]),
        pltpu.make_async_copy(down_hbm, down_ref, sems.at[2]),
    ]
    for weight_copy in copies:
        weight_copy.start()
    width = gate_ref.shape[0]
    parts = []
    copies[0].wait()
    for rows_ref in (other_ref, kept_ref):
        parts.append(jnp.dot(rows_ref[:, :width], gate_ref[...], preferred_element_type=jnp.float32))
    copies[1].wait()
    hiddens = []
    for rows_ref, gate in zip((other_ref, kept_ref), parts):
        upward = jnp.dot(rows_ref[:, :width], up_ref[...], preferred_element_type=jnp.float32)
        hiddens.append((gate / (1.0 + jnp.exp(-gate)) * upward).astype(jnp.bfloat16))
    copies[2].wait()
    for rows_ref, hidden, out_ref in zip((other_ref, kept_ref), hiddens, (other_out, kept_out)):
        side = rows_ref[:, width:].astype(jnp.float32)
        line = lax.broadcasted_iota(jnp.int32, side.shape, 1)
        mine = (line == label_ref[0]) | (line == label_ref[0] + experts)
        mine = mine | (line == label_ref[0] + 2 * experts)
        weight = jnp.sum(jnp.where(mine, side, 0.0), axis=1, keepdims=True)
        total = jnp.dot(hidden, down_ref[...], preferred_element_type=jnp.float32) * weight
        out_ref[...] = total.astype(out_ref.dtype)


def expert_rows(label, kept, other, gate, up, down, experts):
    return pl.pallas_call(
        functools.partial(expert_body, experts),
        out_shape=(
            jax.ShapeDtypeStruct((kept.shape[0], gate.shape[0]), jnp.float32),
            jax.ShapeDtypeStruct((other.shape[0], gate.shape[0]), jnp.bfloat16),
        ),
        in_specs=[pl.BlockSpec(memory_space=pltpu.SMEM)]
        + [pl.BlockSpec(memory_space=pltpu.VMEM)] * 2
        + [pl.BlockSpec(memory_space=pltpu.HBM)] * 3,
        scratch_shapes=[
            pltpu.VMEM(gate.shape, gate.dtype),
            pltpu.VMEM(up.shape, up.dtype),
            pltpu.VMEM(down.shape, down.dtype),
            pltpu.SemaphoreType.DMA((3,)),
        ],
        compiler_params=pltpu.CompilerParams(vmem_limit_bytes=56 << 20),
        cost_estimate=pl.CostEstimate(flops=0, bytes_accessed=0, transcendentals=0),
        name="expert_rows",
    )(label, kept, other, gate, up, down)


def attend_body(plan_ref, query_ref, high_ref, pages_ref, out_ref, context, held, packed, sems, out_sem):
    requests, each, pairs, width = context.shape
    rows = query_ref.shape[1]
    contract = (((1,), (1,)), ((), ()))

    for r in range(requests):

        def begin(i, carry, r=r):
            pltpu.make_async_copy(
                pages_ref.at[plan_ref[requests + r * each + i]], context.at[r, i], sems.at[r]
            ).start()
            return carry

        lax.fori_loop(0, each, begin, 0, unroll=4)

    columns = each * pairs
    draft = lax.broadcasted_iota(jnp.int32, (rows, columns), 0) % DRAFT
    early = 2 * lax.broadcasted_iota(jnp.int32, (rows, columns), 1) - draft

    def score(r):
        pltpu.make_async_copy(context.at[r], context.at[r], sems.at[r]).wait()
        block = context[r].reshape(columns, width)
        low = query_ref[r]
        high = high_ref[r]
        even = lax.dot_general(
            low, block[:, :HALF], contract, preferred_element_type=jnp.float32
        )
        odd = lax.dot_general(
            high, block[:, width - HALF :], contract, preferred_element_type=jnp.float32
        )
        return even, odd

    scored = score(0)
    for r in range(requests):
        even, odd = scored
        if r + 1 < requests:
            scored = score(r + 1)
        limit = plan_ref[r]
        even = jnp.where(early <= limit, even, masked_score)
        odd = jnp.where(early < limit, odd, masked_score)
        highest = jnp.max(jnp.maximum(even, odd), axis=-1, keepdims=True)
        even = jnp.exp2((even - highest) * exponent_scale)
        odd = jnp.exp2((odd - highest) * exponent_scale)
        total = jnp.sum(even + odd, axis=-1, keepdims=True)
        block = context[r].reshape(columns, width)
        latent = jnp.dot(
            even.astype(jnp.bfloat16), block[:, :KV], preferred_element_type=jnp.float32
        )
        other = jnp.dot(
            odd.astype(jnp.bfloat16), block[:, width - HALF :], preferred_element_type=jnp.float32
        )
        latent = (latent + other[:, SHIFT : SHIFT + KV]) * (1.0 / total)
        for h in range(rows // DRAFT):
            held[r * DRAFT : (r + 1) * DRAFT, h * KV : (h + 1) * KV] = latent[
                h * DRAFT : (h + 1) * DRAFT, :
            ]
    span = held.shape[1] // PIECES
    for piece in range(PIECES):
        lanes = slice(piece * span, (piece + 1) * span)
        packed[:, lanes] = held[:, lanes].astype(packed.dtype)
        pltpu.make_async_copy(packed.at[:, lanes], out_ref.at[:, lanes], out_sem).start()
    pltpu.make_async_copy(packed, out_ref, out_sem).wait()


def attend(plan, query, high, pages, each):
    requests, rows, _ = query.shape
    _, pairs, width = pages.shape
    out = (requests * DRAFT, (rows // DRAFT) * KV)
    return pl.pallas_call(
        attend_body,
        out_shape=jax.ShapeDtypeStruct(out, jnp.bfloat16),
        in_specs=[
            pl.BlockSpec(memory_space=pltpu.SMEM),
            pl.BlockSpec(memory_space=pltpu.VMEM),
            pl.BlockSpec(memory_space=pltpu.VMEM),
            pl.BlockSpec(memory_space=pltpu.HBM),
        ],
        out_specs=pl.BlockSpec(memory_space=pltpu.HBM),
        scratch_shapes=[
            pltpu.VMEM((requests, each, pairs, width), pages.dtype),
            pltpu.VMEM(out, jnp.float32),
            pltpu.VMEM(out, jnp.bfloat16),
            pltpu.SemaphoreType.DMA((requests,)),
            pltpu.SemaphoreType.DMA,
        ],
        compiler_params=pltpu.CompilerParams(vmem_limit_bytes=50 << 20),
        name="attend_pages",
    )(plan, query, high, pages)


def local(
    queries,
    page_pool,
    page_table,
    serving,
    context_len,
    residual,
    routes,
    route_scores,
    w_gate,
    w_up,
    w_down,
):
    group = ("ep", "sub")
    peers = lax.axis_size(group)
    device = lax.axis_index(group)
    rows_dev, width = residual.shape
    requests_dev = rows_dev // DRAFT
    pages_each = page_table.shape[1]
    pool_pages = page_pool.shape[0]
    listed = requests_dev * pages_each
    fetched = listed // peers
    n_requests = serving.shape[0]

    n_ep = lax.axis_size("ep")
    experts = n_ep // 2
    far, near = peers // 2, peers // 4

    outgoing, packed = stage_pages(
        group,
        page_table.T,
        serving.reshape(1, -1),
        page_pool,
        residual,
        routes.T,
        route_scores.T,
        peers,
        listed,
        experts,
    )
    across = [exchange(packed, group, bit) for bit in (far, far | near, near)]
    pairs = outgoing.shape[1]
    arrived = lax.all_to_all(
        outgoing.reshape(peers, fetched, pairs, 2 * LAT), group, split_axis=0, concat_axis=0, tiled=True
    )

    kept = join_rows([packed, across[0], across[2], across[1]])
    bit = near // 2
    while bit > 1:
        kept = jnp.concatenate([kept, exchange(kept, group, bit)], axis=0)
        bit //= 2
    kept, queries = lax.optimization_barrier((kept, queries))
    other = exchange(kept, group, 1)
    heads = queries.reshape(requests_dev, DRAFT, HEADS, LAT).transpose(0, 2, 1, 3)
    heads = heads.reshape(requests_dev, HEADS * DRAFT, LAT)
    query = [jnp.pad(heads, ((0, 0), (0, 0), sides)) for sides in ((0, SHIFT), (SHIFT, 0))]
    label = (lax.axis_index("ep") // 2).reshape(1)
    mixed, leaving = expert_rows(label, kept, other, w_gate[0], w_up[0], w_down[0], experts)
    bit = 1
    while True:
        last = exchange(leaving, group, bit)
        bit *= 2
        if bit == peers:
            break
        mixed = mixed + last.astype(jnp.float32)
        if bit == 2:
            mixed, query = lax.optimization_barrier((mixed, query))
        half = mixed.shape[0] // 2
        leaving = mixed[half:].astype(jnp.bfloat16)
        mixed = mixed[:half]

    served = lax.dynamic_slice_in_dim(serving, device * requests_dev, requests_dev)
    slots = jnp.arange(n_requests, dtype=jnp.int32)
    chosen = served[:, None] == slots[None, :]
    own_list = jnp.sum(jnp.where(chosen[:, :, None], page_table[None], 0), axis=1)
    own_list = own_list.reshape(-1) // pool_pages
    position = jnp.arange(listed, dtype=jnp.int32)
    same = (own_list[:, None] == own_list[None, :]) & (position[None, :] < position[:, None])
    place = own_list * fetched + jnp.sum(same.astype(jnp.int32), axis=1)
    limits = jnp.sum(jnp.where(chosen, context_len[None, :], 0), axis=1) - DRAFT
    plan = jnp.concatenate([limits, place])
    mixed = residual.astype(jnp.float32) + mixed
    latent_out = attend(plan, *query, arrived.reshape(listed, pairs, 2 * LAT), pages_each)
    latent_out, last, mixed = lax.optimization_barrier((latent_out, last, mixed))
    moe_out = (mixed + last.astype(jnp.float32)).astype(jnp.bfloat16)
    return (latent_out, moe_out)


def solution(mesh):
    placed = (
        P(("rep", "ep", "sub"), None),
        P(("rep", "ep", "sub"), None),
        P("rep", None),
        P("rep"),
        P("rep"),
        P(("rep", "ep", "sub"), None),
        P(("rep", "ep", "sub"), None),
        P(("rep", "ep", "sub"), None),
        P("ep", None, "sub"),
        P("ep", None, "sub"),
        P("ep", "sub", None),
    )
    return jax.shard_map(
        local,
        mesh=mesh,
        in_specs=placed,
        out_specs=(P(("rep", "ep", "sub"), None), P(("rep", "ep", "sub"), None)),
        check_vma=False,
    )
```
